512 devices in a mesh: pair: 64 (over z, y), ka: 8 (over x, core).
Axes of the slice: x: 4, y: 8, z: 8, core: 2. Of those that a mesh axis runs over, the one named last changes fastest.
Arguments:
- amplitude: bfloat16 [24576, 128, 128], P(('pair', 'ka')), may hold values from -6 to 6
- slot_owner: int32 [24576], P(('pair', 'ka')), may hold values from 0 to 63, as said below
- slot_tile: int32 [24576], P(('pair', 'ka')), may hold values from 0 to 2
- integrals: bfloat16 [1536, 128, 256], P(('pair', 'ka')), may hold values from -0.109375 to 0.109375
- tile_mask: int32 [1536, 2], P(('pair', 'ka')), may hold values 0 or 1
Outputs:
- residual: float32 [8192, 256], P(('pair', 'ka'))
The draws below stay inside these ranges and needn't reach their ends.
Inputs may be any that keep to these rules, and one draw needn't show every extreme that they name: Among the 48 amplitude tiles of one device no two have the same slot_owner and slot_tile together.
All inputs are finite; a program needn't handle non-finite values. No bound on the sum of `tile_mask` on one device may be relied on, other than what follows from the above.
Results may differ from the reference program's by a relative error of at most 0.0003.
Values may be sent and summed in bfloat16 or wider, within the bound.
A program may use at most 64 MiB of HBM per device.

```python
import jax
import jax.numpy as jnp
from jax import lax

TILE = 128
AB = 2
CD_DEV = 3
OWNERS = 64
SPLITS = 8
NS = 48
SLOTS = 24576
CDT = 1536
ROWS = 8192


def choose_pairs(key):
    blocks = SLOTS // NS
    owner_total = ROWS // TILE
    candidates = owner_total * CD_DEV
    popular = jax.random.randint(jax.random.fold_in(key, 101), (owner_total,), 0, 4)
    weight_of = jnp.repeat(popular, CD_DEV)
    order = jnp.arange(candidates, dtype=jnp.int32)

    def one_block(block_index):
        block_key = jax.random.fold_in(jax.random.fold_in(key, 202), block_index)
        noise = jax.random.randint(block_key, (candidates,), 0, 65536)
        forced = block_index % owner_total * CD_DEV + (block_index + block_index // owner_total) % CD_DEV
        scores = (weight_of * 16384 + noise + jnp.where(order == forced, 200000, 0)) * candidates + order
        values, chosen = lax.top_k(scores, NS)
        return chosen
    chosen = jax.vmap(one_block)(jnp.arange(blocks, dtype=jnp.int32))
    return chosen.reshape(-1).astype(jnp.int32)


def draw_slot_owner(key, part):
    pairs = choose_pairs(key)
    return (pairs // CD_DEV).astype(jnp.int32)


def draw_slot_tile(key, part):
    pairs = choose_pairs(key)
    return (pairs % CD_DEV).astype(jnp.int32)


def place_ends(result, key, low, top_value):
    extent = result.shape
    index_at = [jax.random.randint(jax.random.fold_in(key, axis), (), 0, extent[axis]) for axis in range(len(extent))]
    result = result.at[tuple(index_at)].set(low)
    longest = extent.index(max(extent))
    index_at[longest] = (index_at[longest] + 1) % extent[longest]
    return result.at[tuple(index_at)].set(top_value)


def block_scale(own_key, extent, split, low, largest):
    gain = 1.0
    for dim, shards_of in split:
        draws = jax.random.uniform(jax.random.fold_in(jax.random.fold_in(own_key, 6), dim), (shards_of,), jnp.float32, low / len(split), largest / len(split))
        gain = gain * jnp.repeat(jnp.exp(draws), extent[dim] // shards_of).reshape((-1,) + (1,) * (len(extent) - 1 - dim))
    return gain


def normal_values(key, shape, width, limit, pieces=(), held_as=jnp.bfloat16):
    drawn = jax.random.normal(key, shape, jnp.float32) * width
    if len(pieces) > 0:
        drawn = block_scale(key, shape, pieces, -0.22, 0.18) * drawn
    return jnp.clip(drawn, min=-limit, max=limit).astype(held_as)


def setup_inputs(seed: int = 0) -> dict:
    splits = jax.random.split(jax.random.key(seed), 6)
    amplitude = normal_values(splits[0], (SLOTS, TILE, TILE), 1.0, 6.0, ((0, 512),))
    slot_owner = draw_slot_owner(jax.random.fold_in(splits[5], 71), 0)
    slot_tile = draw_slot_tile(jax.random.fold_in(splits[5], 71), 0)
    integrals = normal_values(splits[3], (CDT, TILE, AB * TILE), (NS * TILE // 2) ** -0.5, 0.109375, ((0, 512),))
    tile_mask = place_ends((jax.random.randint(splits[4], (CDT, AB), 0, 2) < 1).astype(jnp.int32), jax.random.fold_in(splits[4], 1), 0, 1)
    return {"amplitude": amplitude, "slot_owner": slot_owner, "slot_tile": slot_tile, "integrals": integrals, "tile_mask": tile_mask}


def reference(amplitude, slot_owner, slot_tile, integrals, tile_mask):
    masked = (integrals.reshape(CDT, TILE, AB, TILE) * tile_mask.astype(jnp.bfloat16)[:, None, :, None]).reshape(CDT, TILE, AB * TILE)
    per_row = SPLITS * NS
    split_index = ((jnp.arange(SLOTS, dtype=jnp.int32) // NS) % SPLITS).astype(jnp.int32)
    tile_index = ((slot_owner * SPLITS + split_index) * CD_DEV + slot_tile).astype(jnp.int32)
    grouped = amplitude.reshape(OWNERS, per_row, TILE, TILE)
    indices = tile_index.reshape(OWNERS, per_row)

    def one_row(operands):
        tiles_here, index_here = operands
        chosen = jnp.take(masked, index_here, axis=0).astype(jnp.float32)
        return jnp.einsum('sij,sjk->ik', tiles_here.astype(jnp.float32), chosen)

    residual = lax.map(one_row, (grouped, indices))
    return residual.reshape(ROWS, AB * TILE)
```

```python
import functools

import jax
import jax.numpy as jnp
from jax import lax
from jax.experimental import pallas as pl
from jax.experimental.pallas import tpu as pltpu
from jax.sharding import PartitionSpec as P

MESH = pl.DeviceIdType.MESH

TILE = 128
AB = 2
HELD = 3
NS = 48
RING = 8
KA = 8
MINE = HELD * AB
GROUP = RING * MINE
HALF = MINE // 2
ROWS = TILE // KA

CAPS = (30, 28, 24, 12)
HOPS = len(CAPS)
CUTS = (0,) + CAPS[::-1]


def region(sign, hop):
    return GROUP + sign * sum(CAPS) + sum(CAPS[: hop - 1])


ZERO_SLOT = GROUP + 2 * sum(CAPS)
SLOTS = ZERO_SLOT + 1


def kernel(
    owner_ref, tile_ref, mask_ref, integrals_ref, amplitude_ref,
    out_ref, flag_ref,
    amp, group, lists, pool, need_tx, need_rx, mask_rx, order, tab_tx, tab_rx, vote_tx, vote_rx,
    order_s, tab_s, index_s, total, part_tx, part_rx,
    local_sem, one_send, one_recv, two_send, two_recv, need_send, need_recv, mask_send, mask_recv,
    tab_send, tab_recv, vote_send, vote_recv, part_send, part_recv,
):
    pair, ka = lax.axis_index("pair"), lax.axis_index("ka")
    core = lax.rem(ka, 2)
    high, low = lax.div(pair, RING), lax.rem(pair, RING)
    u = high + core * (low - high)
    v = low + core * (high - low)
    stride_u, stride_v = RING - (RING - 1) * core, 1 + (RING - 1) * core

    def on_first(step):
        return (lax.rem(u + step + RING, RING) * stride_u + v * stride_v, ka)

    def on_second(step):
        return (u * stride_u + lax.rem(v + step + RING, RING) * stride_v, ka)

    def on_ka(step):
        return (pair, lax.rem(ka + step, KA))

    barrier = pltpu.get_barrier_semaphore()
    for step in range(1, RING):
        for there in (on_first(step), on_second(step), on_ka(step)):
            pl.semaphore_signal(barrier, inc=1, device_id=there, device_id_type=MESH)

    amp_copy = pltpu.make_async_copy(amplitude_ref, amp, local_sem.at[0])
    amp_copy.start()

    for t in range(HELD):
        for a in range(AB):
            block = integrals_ref[t, :, a * TILE : (a + 1) * TILE].astype(jnp.float32)
            scale = mask_ref[t, a].astype(jnp.float32)
            group[u * MINE + t * AB + a] = (block * scale).astype(jnp.bfloat16)

    lane = lax.broadcasted_iota(jnp.int32, (8, TILE), 1)
    own_mask = jnp.zeros((8, TILE), jnp.float32)
    for t in range(HELD):
        for a in range(AB):
            here = lane == u * MINE + t * AB + a
            own_mask = jnp.where(here, mask_ref[t, a].astype(jnp.float32), own_mask)
    mask_rx[0] = own_mask

    def source_of(s):
        owner = owner_ref[s]
        oh, ol = owner // RING, lax.rem(owner, RING)
        return oh + core * (ol - oh), ol + core * (oh - ol), tile_ref[s]

    code = lax.broadcasted_iota(jnp.int32, (RING, 8, TILE), 0) * TILE + lax.broadcasted_iota(
        jnp.int32, (RING, 8, TILE), 2
    ) // AB

    def mark(s, seen):
        su, sv, st = source_of(s)
        distance = lax.rem(sv - v + RING, RING)
        return jnp.where(code == distance * TILE + su * HELD + st, 1.0, seen)

    need_tx[...] = lax.fori_loop(0, NS, mark, jnp.zeros((RING, 8, TILE), jnp.float32))

    pool[ZERO_SLOT] = jnp.zeros((TILE, TILE), jnp.bfloat16)

    pl.semaphore_wait(barrier, 3 * (RING - 1))

    def remote(src, dst, send, recv, there):
        return pltpu.make_async_remote_copy(
            src_ref=src, dst_ref=dst, send_sem=send, recv_sem=recv, device_id=there, device_id_type=MESH
        )

    def first(sign, hop, chunk):
        behind = lax.rem(u + (hop - 1 if sign else RING - hop + 1), RING)
        ref = group.at[pl.ds(behind * MINE + chunk * HALF, HALF)]
        number = (sign * 4 + hop - 1) * 2 + chunk
        return remote(ref, ref, one_send.at[number], one_recv.at[number], on_first(-1 if sign else 1))

    def first_arrival(sign, hop, chunk):
        behind = lax.rem(u + (hop if sign else RING - hop), RING)
        ref = group.at[pl.ds(behind * MINE + chunk * HALF, HALF)]
        number = (sign * 4 + hop - 1) * 2 + chunk
        return remote(ref, ref, one_send.at[number], one_recv.at[number], on_first(-1 if sign else 1))

    need_copies = [
        remote(need_tx.at[j], need_rx.at[j], need_send.at[j], need_recv.at[j], on_second(j)) for j in range(1, RING)
    ]
    mask_copies = [
        remote(mask_rx.at[0], mask_rx.at[j], mask_send.at[j], mask_recv.at[j], on_first(j)) for j in range(1, RING)
    ]
    sent = []

    def start(copy):
        copy.start()
        sent.append(copy)

    for sign in range(2):
        start(first(sign, 1, 0))
    for copy in need_copies + mask_copies:
        start(copy)
    for sign in range(2):
        start(first(sign, 1, 1))
    for hop in (2, 3):
        for chunk in range(2):
            for sign in range(2):
                first_arrival(sign, hop - 1, chunk).wait_recv()
                start(first(sign, hop, chunk))

    for copy in need_copies + mask_copies:
        copy.wait_recv()
    mask = mask_rx[0]
    for j in range(1, RING):
        mask = jnp.maximum(mask, mask_rx[j])
    even = (lane % 2) == 0
    flane = lane.astype(jnp.float32)
    wide_lane = lax.broadcasted_iota(jnp.int32, (GROUP, TILE), 1)
    wide_row = lax.broadcasted_iota(jnp.int32, (GROUP, TILE), 0)
    ranks = []
    over = jnp.zeros((8, TILE), jnp.float32)
    for sign in range(2):
        far = jnp.zeros((8, TILE), jnp.float32)
        for distance in range(1, HOPS + 1):
            needed = need_rx[distance if sign else RING - distance] * mask
            if distance == HOPS:
                needed = jnp.where(even == (sign == 0), needed, 0.0)
            far = jnp.where(needed > 0.0, float(distance), far)
        for hop in range(1, HOPS + 1):
            count = jnp.sum(jnp.where(far >= float(hop), 1.0, 0.0), axis=1, keepdims=True)
            over = jnp.maximum(over, jnp.where(count > float(CAPS[hop - 1]), 1.0, 0.0))
        key = far * float(TILE) + (float(TILE - 1) - flane)
        key_row = jnp.broadcast_to(key[0:1], (GROUP, TILE))
        key_col = jnp.sum(jnp.where(wide_lane == wide_row, key_row, 0.0), axis=1, keepdims=True)
        rank_row = jnp.sum(jnp.where(key_col > key_row, 1.0, 0.0), axis=0, keepdims=True)
        rank_col = jnp.sum(jnp.where(key_row > key_col, 1.0, 0.0), axis=1, keepdims=True)
        chosen = jnp.where(rank_col == wide_lane.astype(jnp.float32), wide_row.astype(jnp.float32), 0.0)
        inverse = jnp.sum(chosen, axis=0, keepdims=True)
        order[sign] = jnp.broadcast_to(inverse, (8, TILE)).astype(jnp.int32)
        ranks.append(jnp.broadcast_to(rank_row, (8, TILE)))
    order_copy = pltpu.make_async_copy(order, order_s, local_sem.at[1])
    order_copy.start()

    sub = lax.broadcasted_iota(jnp.int32, (8, TILE), 0)
    for j in range(1, RING):
        right = ranks[0] + float(region(0, min(j, HOPS)))
        left = ranks[1] + float(region(1, min(RING - j, HOPS)))
        slot = right if j < HOPS else left if j > HOPS else jnp.where(even, right, left)
        slot = jnp.where(mask > 0.0, slot, float(ZERO_SLOT))
        tab_tx[j] = jnp.where(sub == 0, slot, over).astype(jnp.int32)
    tab_copies = [
        remote(tab_tx.at[j], tab_rx.at[j], tab_send.at[j], tab_recv.at[j], on_second(j)) for j in range(1, RING)
    ]
    tab_rx[0] = jnp.where(sub == 0, lane, over.astype(jnp.int32))

    for sign in range(2):
        first_arrival(sign, 3, sign).wait_recv()
        start(first(sign, 4, sign))
    for sign in range(2):
        first_arrival(sign, 3, 1 - sign).wait_recv()
    for copy in tab_copies:
        start(copy)
    order_copy.wait()
    for sign in range(2):
        first_arrival(sign, 4, sign).wait_recv()

    def second(sign, hop, piece):
        begin, size = CUTS[piece], CUTS[piece + 1] - CUTS[piece]
        if hop == 1:
            src = lists.at[sign, pl.ds(begin, size)]
        else:
            src = pool.at[pl.ds(region(sign, hop - 1) + begin, size)]
        dst = pool.at[pl.ds(region(sign, hop) + begin, size)]
        number = (sign * HOPS + hop - 1) * HOPS + piece
        return remote(src, dst, two_send.at[number], two_recv.at[number], on_second(-1 if sign else 1))

    for piece in range(HOPS):
        for sign in range(2):

            def pick(r, carry, sign=sign):
                lists[sign, r] = group[jnp.clip(order_s[sign, 0, r], 0, GROUP - 1)]
                return carry

            lax.fori_loop(CUTS[piece], CUTS[piece + 1], pick, 0)
            start(second(sign, 1, piece))
    own_copy = pltpu.make_async_copy(group, pool.at[pl.ds(0, GROUP)], local_sem.at[2])
    own_copy.start()

    for copy in tab_copies:
        copy.wait_recv()
    tab_copy = pltpu.make_async_copy(tab_rx, tab_s, local_sem.at[3])
    tab_copy.start()
    vote = tab_rx[0]
    for j in range(1, RING):
        vote = jnp.maximum(vote, tab_rx[j])
    vote_tx[...] = jnp.broadcast_to(vote[1:2], (8, TILE))
    vote_copies = [
        remote(vote_tx, vote_rx.at[j], vote_send.at[j], vote_recv.at[j], on_first(j)) for j in range(1, RING)
    ]
    for copy in vote_copies:
        start(copy)

    tab_copy.wait()

    def locate(s, carry):
        su, sv, st = source_of(s)
        distance = lax.rem(v - sv + RING, RING)
        for a in range(AB):
            slot = tab_s[distance, 0, su * MINE + st * AB + a]
            index_s[s * AB + a] = jnp.clip(slot, 0, ZERO_SLOT)
        return carry

    lax.fori_loop(0, NS, locate, 0)

    for hop in range(2, HOPS + 1):
        for piece in range(HOPS - hop + 1):
            for sign in range(2):
                second(sign, hop - 1, piece).wait_recv()
                start(second(sign, hop, piece))
    for copy in vote_copies:
        copy.wait_recv()
    vote = vote_tx[...]
    for j in range(1, RING):
        vote = jnp.maximum(vote, vote_rx[j])
    vote_wide = jnp.concatenate([vote, vote], axis=1).astype(jnp.float32)
    own_copy.wait()
    amp_copy.wait()
    for hop in range(1, HOPS + 1):
        for sign in range(2):
            second(sign, hop, HOPS - hop).wait_recv()

    total[...] = jnp.zeros_like(total)

    def multiply(i, carry):
        left = jnp.concatenate([amp[2 * i], amp[2 * i + 1]], axis=1)
        rows = [
            jnp.concatenate([pool[index_s[4 * i + 2 * h]], pool[index_s[4 * i + 2 * h + 1]]], axis=1)
            for h in range(2)
        ]
        total[...] += jnp.dot(left, jnp.concatenate(rows, axis=0), preferred_element_type=jnp.float32)
        return carry

    lax.fori_loop(0, NS // 2, multiply, 0)

    for q in range(KA):
        part_tx[q, 0:ROWS] = total[q * ROWS : (q + 1) * ROWS]
        part_tx[q, ROWS : ROWS + 8] = vote_wide
    part_copies = [
        remote(part_tx.at[lax.rem(ka + j, KA)], part_rx.at[j], part_send.at[j], part_recv.at[j], on_ka(j))
        for j in range(1, KA)
    ]
    for copy in part_copies:
        start(copy)
    result = part_tx[ka, 0:ROWS]
    for copy in part_copies:
        copy.wait_recv()
    vote = vote_wide
    for j in range(1, KA):
        result += part_rx[j, 0:ROWS]
        vote = jnp.maximum(vote, part_rx[j, ROWS : ROWS + 8])
    out_ref[...] = result
    flag_ref[...] = vote[:, 0:TILE]
    for copy in sent:
        copy.wait_send()


def ladder(amplitude, slot_owner, slot_tile, integrals, tile_mask):
    scratch = [
        pltpu.VMEM((NS, TILE, TILE), jnp.bfloat16),
        pltpu.VMEM((GROUP, TILE, TILE), jnp.bfloat16),
        pltpu.VMEM((2, CAPS[0], TILE, TILE), jnp.bfloat16),
        pltpu.VMEM((SLOTS, TILE, TILE), jnp.bfloat16),
        pltpu.VMEM((RING, 8, TILE), jnp.float32),
        pltpu.VMEM((RING, 8, TILE), jnp.float32),
        pltpu.VMEM((RING, 8, TILE), jnp.float32),
        pltpu.VMEM((2, 8, TILE), jnp.int32),
        pltpu.VMEM((RING, 8, TILE), jnp.int32),
        pltpu.VMEM((RING, 8, TILE), jnp.int32),
        pltpu.VMEM((8, TILE), jnp.int32),
        pltpu.VMEM((RING, 8, TILE), jnp.int32),
        pltpu.SMEM((2, 8, TILE), jnp.int32),
        pltpu.SMEM((RING, 8, TILE), jnp.int32),
        pltpu.SMEM((NS * AB,), jnp.int32),
        pltpu.VMEM((TILE, AB * TILE), jnp.float32),
        pltpu.VMEM((KA, ROWS + 8, AB * TILE), jnp.float32),
        pltpu.VMEM((KA, ROWS + 8, AB * TILE), jnp.float32),
        pltpu.SemaphoreType.DMA((4,)),
        pltpu.SemaphoreType.DMA((16,)),
        pltpu.SemaphoreType.DMA((16,)),
        pltpu.SemaphoreType.DMA((2 * HOPS * HOPS,)),
        pltpu.SemaphoreType.DMA((2 * HOPS * HOPS,)),
    ] + [pltpu.SemaphoreType.DMA((RING,)) for _ in range(10)]
    smem, vmem = pl.BlockSpec(memory_space=pltpu.SMEM), pl.BlockSpec(memory_space=pltpu.VMEM)
    return pl.pallas_call(
        kernel,
        out_shape=(
            jax.ShapeDtypeStruct((ROWS, AB * TILE), jnp.float32),
            jax.ShapeDtypeStruct((8, TILE), jnp.float32),
        ),
        in_specs=[smem, smem, smem, vmem, pl.BlockSpec(memory_space=pl.ANY)],
        out_specs=(vmem, vmem),
        scratch_shapes=scratch,
        compiler_params=pltpu.CompilerParams(
            collective_id=0, has_side_effects=True, vmem_limit_bytes=32 * 1024 * 1024
        ),
    )(slot_owner, slot_tile, tile_mask, integrals, amplitude)


def dense(amplitude, slot_owner, slot_tile, integrals, tile_mask):
    held, edge, columns = integrals.shape
    bands = columns // edge
    masked = (
        integrals.reshape(held, edge, bands, edge) * tile_mask.astype(jnp.bfloat16)[:, None, :, None]
    ).reshape(held, edge, columns)
    everything = lax.all_gather(masked, "pair", axis=0, tiled=True)
    chosen = jnp.take(everything, slot_owner * held + slot_tile, axis=0)
    rows = jnp.einsum("sij,sjk->ik", amplitude, chosen, preferred_element_type=jnp.float32)
    return lax.psum_scatter(rows, "ka", scatter_dimension=0, tiled=True)


def local(amplitude, slot_owner, slot_tile, integrals, tile_mask):
    result, flag = ladder(amplitude, slot_owner, slot_tile, integrals, tile_mask)
    return lax.cond(
        flag[0, 0] > 0.0,
        lambda: dense(amplitude, slot_owner, slot_tile, integrals, tile_mask),
        lambda: result,
    )


def solution(mesh):
    in_specs = (
        P(("pair", "ka"), None, None),
        P(("pair", "ka")),
        P(("pair", "ka")),
        P(("pair", "ka"), None, None),
        P(("pair", "ka"), None),
    )
    out_specs = P(("pair", "ka"), None)
    return jax.shard_map(local, mesh=mesh, in_specs=in_specs, out_specs=out_specs, check_vma=False)
```

```python
import functools

import jax
import jax.numpy as jnp
from jax import lax
from jax.experimental import pallas as pl
from jax.experimental.pallas import tpu as pltpu
from jax.sharding import PartitionSpec as P

MESH = pl.DeviceIdType.MESH

TILE = 128
AB = 2
HELD = 3
NS = 48
RING = 8
KA = 8
MINE = HELD * AB
GROUP = RING * MINE
HALF = MINE // 2
STEP = 8
ROWS = TILE // KA

CAPS = (30, 29, 25, 12)
HOPS = len(CAPS)
LONGEST = 8


def cut_lists():
    pieces = []
    for hops, (begin, end) in zip(range(HOPS, 0, -1), zip((0,) + CAPS[::-1], CAPS[::-1])):
        count = -(-(end - begin) // LONGEST)
        for i in range(count):
            left, right = (end - begin) * i // count, (end - begin) * (i + 1) // count
            pieces.append((begin + left, right - left, hops))
    return pieces


PIECES = cut_lists()


def region(sign, hop):
    return GROUP + sign * sum(CAPS) + sum(CAPS[: hop - 1])


ZERO_SLOT = GROUP + 2 * sum(CAPS)
SLOTS = ZERO_SLOT + 1


def kernel(
    owner_ref, tile_ref, mask_ref, integrals_ref, amplitude_ref,
    out_ref, flag_ref,
    amp, group, lists, pool, need_tx, need_rx, mask_rx, order, tab_tx, tab_rx, vote_tx, vote_rx,
    order_s, tab_s, index_s, total, part_tx, part_rx,
    local_sem, one_send, one_recv, two_send, two_recv, need_send, need_recv, mask_send, mask_recv,
    tab_send, tab_recv, vote_send, vote_recv, part_send, part_recv,
):
    pair, ka = lax.axis_index("pair"), lax.axis_index("ka")
    core = lax.rem(ka, 2)
    high, low = lax.div(pair, RING), lax.rem(pair, RING)
    u = high + core * (low - high)
    v = low + core * (high - low)
    stride_u, stride_v = RING - (RING - 1) * core, 1 + (RING - 1) * core

    def on_first(step):
        return (lax.rem(u + step + RING, RING) * stride_u + v * stride_v, ka)

    def on_second(step):
        return (u * stride_u + lax.rem(v + step + RING, RING) * stride_v, ka)

    def on_ka(step):
        return (pair, lax.rem(ka + step, KA))

    load_copies = [
        pltpu.make_async_copy(
            integrals_ref.at[:, :, pl.ds(a * TILE, TILE)],
            group.at[pl.ds(u * MINE + a * HELD, HELD)],
            local_sem.at[4 + a],
        )
        for a in range(AB)
    ]
    for copy in load_copies:
        copy.start()

    barrier = pltpu.get_barrier_semaphore()
    for step in range(1, RING):
        for there in (on_first(step), on_second(step), on_ka(step)):
            pl.semaphore_signal(barrier, inc=1, device_id=there, device_id_type=MESH)

    amp_copy = pltpu.make_async_copy(amplitude_ref, amp, local_sem.at[0])
    amp_copy.start()

    lane = lax.broadcasted_iota(jnp.int32, (8, TILE), 1)
    own_mask = jnp.zeros((8, TILE), jnp.float32)
    for t in range(HELD):
        for a in range(AB):
            here = lane == u * MINE + a * HELD + t
            own_mask = jnp.where(here, mask_ref[t : t + 1, a : a + 1].astype(jnp.float32), own_mask)
    mask_rx[0] = own_mask

    def source_of(s):
        owner = owner_ref[s]
        oh, ol = lax.div(owner, RING), lax.rem(owner, RING)
        return oh + core * (ol - oh), ol + core * (oh - ol), tile_ref[s]

    code = lax.broadcasted_iota(jnp.int32, (RING, 8, TILE), 0) * TILE + lax.broadcasted_iota(
        jnp.int32, (RING, 8, TILE), 2
    )

    def mark(s, seen):
        su, sv, st = source_of(s)
        distance = lax.rem(sv - v + RING, RING)
        for a in range(AB):
            seen = jnp.where(code == distance * TILE + su * MINE + a * HELD + st, 1.0, seen)
        return seen

    need_tx[...] = lax.fori_loop(0, NS, mark, jnp.zeros((RING, 8, TILE), jnp.float32))

    pool[ZERO_SLOT] = jnp.zeros((TILE, TILE), jnp.bfloat16)

    for copy in load_copies:
        copy.wait()
    pl.semaphore_wait(barrier, 3 * (RING - 1))

    def remote(src, dst, send, recv, there):
        return pltpu.make_async_remote_copy(
            src_ref=src, dst_ref=dst, send_sem=send, recv_sem=recv, device_id=there, device_id_type=MESH
        )

    def first(sign, hop, chunk):
        behind = lax.rem(u + (hop - 1 if sign else RING - hop + 1), RING)
        ref = group.at[pl.ds(behind * MINE + chunk * HALF, HALF)]
        number = (sign * 4 + hop - 1) * 2 + chunk
        return remote(ref, ref, one_send.at[number], one_recv.at[number], on_first(-1 if sign else 1))

    def first_arrival(sign, hop, chunk):
        behind = lax.rem(u + (hop if sign else RING - hop), RING)
        ref = group.at[pl.ds(behind * MINE + chunk * HALF, HALF)]
        number = (sign * 4 + hop - 1) * 2 + chunk
        return remote(ref, ref, one_send.at[number], one_recv.at[number], on_first(-1 if sign else 1))

    need_copies = [
        remote(need_tx.at[j], need_rx.at[j], need_send.at[j], need_recv.at[j], on_second(j)) for j in range(1, RING)
    ]
    mask_copies = [
        remote(mask_rx.at[0], mask_rx.at[j], mask_send.at[j], mask_recv.at[j], on_first(j)) for j in range(1, RING)
    ]
    sent = []

    def start(copy):
        copy.start()
        sent.append(copy)

    for sign in range(2):
        start(first(sign, 1, 0))
    for copy in need_copies + mask_copies:
        start(copy)
    for sign in range(2):
        start(first(sign, 1, 1))
    def forward(hop):
        for chunk in range(2):
            for sign in range(2):
                first_arrival(sign, hop - 1, chunk).wait_recv()
                start(first(sign, hop, chunk))

    forward(2)

    for copy in need_copies + mask_copies:
        copy.wait_recv()
    mask = mask_rx[0]
    for j in range(1, RING):
        mask = jnp.maximum(mask, mask_rx[j])
    even = (lane % 2) == 0
    flane = lane.astype(jnp.float32)
    wide_lane = lax.broadcasted_iota(jnp.int32, (GROUP, TILE), 1)
    wide_row = lax.broadcasted_iota(jnp.int32, (GROUP, TILE), 0)
    far = []
    for sign in range(2):
        reach = jnp.zeros((8, TILE), jnp.float32)
        for distance in range(1, HOPS):
            needed = need_rx[distance if sign else RING - distance] * mask
            reach = jnp.where(needed > 0.0, float(distance), reach)
        far.append(reach)
    opposite = need_rx[HOPS] * mask > 0.0
    far[0] = jnp.where(jnp.logical_and(opposite, even), float(HOPS), far[0])
    far[1] = jnp.where(jnp.logical_and(opposite, jnp.logical_not(even)), float(HOPS), far[1])
    ranks = []
    over = jnp.zeros((8, TILE), jnp.float32)
    for sign in range(2):
        for hop in range(1, HOPS + 1):
            count = jnp.sum(jnp.where(far[sign] >= float(hop), 1.0, 0.0), axis=1, keepdims=True)
            over = jnp.maximum(over, jnp.where(count > float(CAPS[hop - 1]), 1.0, 0.0))
        key = far[sign] * float(TILE) + (float(TILE - 1) - flane)
        key_row = jnp.broadcast_to(key[0:1], (GROUP, TILE))
        key_col = jnp.sum(jnp.where(wide_lane == wide_row, key_row, 0.0), axis=1, keepdims=True)
        rank_row = jnp.sum(jnp.where(key_col > key_row, 1.0, 0.0), axis=0, keepdims=True)
        rank_col = jnp.sum(jnp.where(key_row > key_col, 1.0, 0.0), axis=1, keepdims=True)
        chosen = jnp.where(rank_col == wide_lane.astype(jnp.float32), wide_row.astype(jnp.float32), 0.0)
        inverse = jnp.sum(chosen, axis=0, keepdims=True)
        order[sign] = jnp.broadcast_to(inverse, (8, TILE)).astype(jnp.int32)
        ranks.append(jnp.broadcast_to(rank_row, (8, TILE)))
    order_copy = pltpu.make_async_copy(order, order_s, local_sem.at[1])
    order_copy.start()
    forward(3)

    sub = lax.broadcasted_iota(jnp.int32, (8, TILE), 0)
    for j in range(1, RING):
        right = ranks[0] + float(region(0, min(j, HOPS)))
        left = ranks[1] + float(region(1, min(RING - j, HOPS)))
        slot = right if j < HOPS else left if j > HOPS else jnp.where(even, right, left)
        slot = jnp.where(mask > 0.0, slot, float(ZERO_SLOT))
        tab_tx[j] = jnp.where(sub == 0, slot, over).astype(jnp.int32)
    tab_copies = [
        remote(tab_tx.at[j], tab_rx.at[j], tab_send.at[j], tab_recv.at[j], on_second(j)) for j in range(1, RING)
    ]
    tab_rx[0] = jnp.where(sub == 0, jnp.where(mask > 0.0, flane, float(ZERO_SLOT)), over).astype(jnp.int32)

    for sign in range(2):
        first_arrival(sign, 3, sign).wait_recv()
        start(first(sign, 4, sign))
    order_copy.wait()
    for sign in range(2):
        first_arrival(sign, 3, 1 - sign).wait_recv()
    for sign in range(2):
        first_arrival(sign, 4, sign).wait_recv()

    def second(sign, hop, piece):
        begin, size, _ = PIECES[piece]
        if hop == 1:
            src = lists.at[sign, pl.ds(begin, size)]
        else:
            src = pool.at[pl.ds(region(sign, hop - 1) + begin, size)]
        dst = pool.at[pl.ds(region(sign, hop) + begin, size)]
        number = (sign * HOPS + hop - 1) * len(PIECES) + piece
        return remote(src, dst, two_send.at[number], two_recv.at[number], on_second(-1 if sign else 1))

    for piece, (begin, size, _) in enumerate(PIECES):
        for sign in range(2):
            for r in range(begin, begin + size):
                lists[sign, r] = group[jnp.clip(order_s[sign, 0, r], 0, GROUP - 1)]
            start(second(sign, 1, piece))
    for copy in tab_copies:
        start(copy)
    own_copy = pltpu.make_async_copy(group, pool.at[pl.ds(0, GROUP)], local_sem.at[2])
    own_copy.start()

    for copy in tab_copies:
        copy.wait_recv()
    tab_copy = pltpu.make_async_copy(tab_rx, tab_s, local_sem.at[3])
    tab_copy.start()
    vote = tab_rx[0]
    for j in range(1, RING):
        vote = jnp.maximum(vote, tab_rx[j])
    vote_tx[...] = jnp.broadcast_to(vote[1:2], (8, TILE))
    vote_copies = [
        remote(vote_tx, vote_rx.at[j], vote_send.at[j], vote_recv.at[j], on_first(j)) for j in range(1, RING)
    ]
    for copy in vote_copies:
        start(copy)

    tab_copy.wait()

    def locate(s, carry):
        su, sv, st = source_of(s)
        distance = lax.rem(v - sv + RING, RING)
        for a in range(AB):
            slot = tab_s[distance, 0, su * MINE + a * HELD + st]
            index_s[s * AB + a] = jnp.clip(slot, 0, ZERO_SLOT)
        return carry

    lax.fori_loop(0, NS, locate, 0)

    for hop in range(2, HOPS + 1):
        for piece, (_, _, hops) in enumerate(PIECES):
            if hops >= hop:
                for sign in range(2):
                    second(sign, hop - 1, piece).wait_recv()
                    start(second(sign, hop, piece))
    for copy in vote_copies:
        copy.wait_recv()
    vote = vote_tx[...]
    for j in range(1, RING):
        vote = jnp.maximum(vote, vote_rx[j])
    vote_wide = jnp.concatenate([vote, vote], axis=1).astype(jnp.float32)
    own_copy.wait()
    amp_copy.wait()
    for piece, (_, _, hops) in enumerate(PIECES):
        for sign in range(2):
            second(sign, hops, piece).wait_recv()

    total[...] = jnp.zeros_like(total)

    def multiply(i, carry):
        tiles = [amp[STEP * i + j] for j in range(STEP)]
        bands = [
            jnp.concatenate([pool[index_s[(STEP * i + j) * AB + a]] for j in range(STEP)], axis=0) for a in range(AB)
        ]
        total[...] += jnp.dot(
            jnp.concatenate(tiles, axis=1), jnp.concatenate(bands, axis=1), preferred_element_type=jnp.float32
        )
        return carry

    lax.fori_loop(0, NS // STEP, multiply, 0)

    for q in range(KA):
        part_tx[q, 0:ROWS] = total[q * ROWS : (q + 1) * ROWS]
        part_tx[q, ROWS : ROWS + 8] = vote_wide
    part_copies = [
        remote(part_tx.at[lax.rem(ka + j, KA)], part_rx.at[j], part_send.at[j], part_recv.at[j], on_ka(j))
        for j in range(1, KA)
    ]
    for copy in part_copies:
        copy.start()
    for copy in sent:
        copy.wait_send()
    result = part_tx[ka, 0:ROWS]
    for copy in part_copies:
        copy.wait_recv()
    vote = vote_wide
    for j in range(1, KA):
        result += part_rx[j, 0:ROWS]
        vote = jnp.maximum(vote, part_rx[j, ROWS : ROWS + 8])
    out_ref[...] = result
    flag_ref[...] = vote[:, 0:TILE]
    for copy in part_copies:
        copy.wait_send()


def ladder(amplitude, slot_owner, slot_tile, integrals, tile_mask):
    scratch = [
        pltpu.VMEM((NS, TILE, TILE), jnp.bfloat16),
        pltpu.VMEM((GROUP, TILE, TILE), jnp.bfloat16),
        pltpu.VMEM((2, CAPS[0], TILE, TILE), jnp.bfloat16),
        pltpu.VMEM((SLOTS, TILE, TILE), jnp.bfloat16),
        pltpu.VMEM((RING, 8, TILE), jnp.float32),
        pltpu.VMEM((RING, 8, TILE), jnp.float32),
        pltpu.VMEM((RING, 8, TILE), jnp.float32),
        pltpu.VMEM((2, 8, TILE), jnp.int32),
        pltpu.VMEM((RING, 8, TILE), jnp.int32),
        pltpu.VMEM((RING, 8, TILE), jnp.int32),
        pltpu.VMEM((8, TILE), jnp.int32),
        pltpu.VMEM((RING, 8, TILE), jnp.int32),
        pltpu.SMEM((2, 8, TILE), jnp.int32),
        pltpu.SMEM((RING, 8, TILE), jnp.int32),
        pltpu.SMEM((NS * AB,), jnp.int32),
        pltpu.VMEM((TILE, AB * TILE), jnp.float32),
        pltpu.VMEM((KA, ROWS + 8, AB * TILE), jnp.float32),
        pltpu.VMEM((KA, ROWS + 8, AB * TILE), jnp.float32),
        pltpu.SemaphoreType.DMA((6,)),
        pltpu.SemaphoreType.DMA((16,)),
        pltpu.SemaphoreType.DMA((16,)),
        pltpu.SemaphoreType.DMA((2 * HOPS * len(PIECES),)),
        pltpu.SemaphoreType.DMA((2 * HOPS * len(PIECES),)),
    ] + [pltpu.SemaphoreType.DMA((RING,)) for _ in range(10)]
    smem, vmem = pl.BlockSpec(memory_space=pltpu.SMEM), pl.BlockSpec(memory_space=pltpu.VMEM)
    hbm = pl.BlockSpec(memory_space=pl.ANY)
    return pl.pallas_call(
        kernel,
        out_shape=(
            jax.ShapeDtypeStruct((ROWS, AB * TILE), jnp.float32),
            jax.ShapeDtypeStruct((8, TILE), jnp.float32),
        ),
        in_specs=[smem, smem, vmem, hbm, hbm],
        out_specs=(vmem, vmem),
        scratch_shapes=scratch,
        compiler_params=pltpu.CompilerParams(
            collective_id=0, has_side_effects=True, vmem_limit_bytes=32 * 1024 * 1024
        ),
    )(slot_owner, slot_tile, tile_mask, integrals, amplitude)


def dense(amplitude, slot_owner, slot_tile, integrals, tile_mask):
    held, edge, columns = integrals.shape
    bands = columns // edge
    masked = (
        integrals.reshape(held, edge, bands, edge) * tile_mask.astype(jnp.bfloat16)[:, None, :, None]
    ).reshape(held, edge, columns)
    everything = lax.all_gather(masked, "pair", axis=0, tiled=True)
    chosen = jnp.take(everything, slot_owner * held + slot_tile, axis=0)
    rows = jnp.einsum("sij,sjk->ik", amplitude, chosen, preferred_element_type=jnp.float32)
    return lax.psum_scatter(rows, "ka", scatter_dimension=0, tiled=True)


def local(amplitude, slot_owner, slot_tile, integrals, tile_mask):
    result, flag = ladder(amplitude, slot_owner, slot_tile, integrals, tile_mask)
    return lax.cond(
        flag[0, 0] > 0.0,
        lambda: dense(amplitude, slot_owner, slot_tile, integrals, tile_mask),
        lambda: result,
    )


def solution(mesh):
    in_specs = (
        P(("pair", "ka"), None, None),
        P(("pair", "ka")),
        P(("pair", "ka")),
        P(("pair", "ka"), None, None),
        P(("pair", "ka"), None),
    )
    out_specs = P(("pair", "ka"), None)
    return jax.shard_map(local, mesh=mesh, in_specs=in_specs, out_specs=out_specs, check_vma=False)
```

```python
import functools

import jax
import jax.numpy as jnp
from jax import lax
from jax.experimental import pallas as pl
from jax.experimental.pallas import tpu as pltpu
from jax.sharding import PartitionSpec as P

MESH = pl.DeviceIdType.MESH

TILE = 128
AB = 2
HELD = 3
NS = 48
RING = 8
KA = 8
MINE = HELD * AB
GROUP = RING * MINE
STEP = 8
ROWS = TILE // KA

HOPS = RING // 2
LONGEST = 8

USUAL = (30, 28, 25, 12)
EVERY = (GROUP, GROUP, GROUP, GROUP // 2)


class Plan:
    def __init__(self, caps):
        self.caps = caps
        self.zero_slot = GROUP + 2 * sum(caps)
        self.slots = self.zero_slot + 1
        self.pieces = []
        for hops, begin, end in zip(range(HOPS, 0, -1), (0,) + caps[::-1], caps[::-1]):
            count = -(-(end - begin) // LONGEST)
            for i in range(count):
                left, right = (end - begin) * i // count, (end - begin) * (i + 1) // count
                self.pieces.append((begin + left, right - left, hops))

    def region(self, sign, hop):
        return GROUP + sign * sum(self.caps) + sum(self.caps[: hop - 1])


def kernel(
    plan, owner_ref, tile_ref, mask_ref, integrals_ref, amplitude_ref,
    out_ref, flag_ref,
    amp, group, lists, pool, need_tx, need_rx, mask_rx, order, tab_tx, tab_rx, vote_tx, vote_rx,
    order_s, tab_s, index_s, total, part_tx, part_rx,
    local_sem, one_send, one_recv, two_send, two_recv, need_send, need_recv, mask_send, mask_recv,
    tab_send, tab_recv, vote_send, vote_recv, part_send, part_recv,
):
    pair, ka = lax.axis_index("pair"), lax.axis_index("ka")
    core = lax.rem(ka, 2)
    high, low = lax.div(pair, RING), lax.rem(pair, RING)
    u = high + core * (low - high)
    v = low + core * (high - low)
    stride_u, stride_v = RING - (RING - 1) * core, 1 + (RING - 1) * core

    def on_first(step):
        return (lax.rem(u + step + RING, RING) * stride_u + v * stride_v, ka)

    def on_second(step):
        return (u * stride_u + lax.rem(v + step + RING, RING) * stride_v, ka)

    def on_ka(step):
        return (pair, lax.rem(ka + step, KA))

    load_copies = [
        pltpu.make_async_copy(
            integrals_ref.at[:, :, pl.ds(a * TILE, TILE)],
            group.at[pl.ds(u * MINE + a * HELD, HELD)],
            local_sem.at[4 + a],
        )
        for a in range(AB)
    ]
    for copy in load_copies:
        copy.start()

    barrier = pltpu.get_barrier_semaphore()
    for step in range(1, RING):
        for there in (on_first(step), on_second(step), on_ka(step)):
            pl.semaphore_signal(barrier, inc=1, device_id=there, device_id_type=MESH)

    amp_copy = pltpu.make_async_copy(amplitude_ref, amp, local_sem.at[0])
    amp_copy.start()

    lane = lax.broadcasted_iota(jnp.int32, (8, TILE), 1)
    own_mask = jnp.zeros((8, TILE), jnp.float32)
    for t in range(HELD):
        for a in range(AB):
            here = lane == u * MINE + a * HELD + t
            own_mask = jnp.where(here, mask_ref[a : a + 1, t : t + 1].astype(jnp.float32), own_mask)
    mask_rx[0] = own_mask

    def source_of(s):
        owner = owner_ref[s]
        oh, ol = lax.div(owner, RING), lax.rem(owner, RING)
        return oh + core * (ol - oh), ol + core * (oh - ol), tile_ref[s]

    code = lax.broadcasted_iota(jnp.int32, (RING, 8, TILE), 0) * TILE + lax.broadcasted_iota(
        jnp.int32, (RING, 8, TILE), 2
    )

    def mark(s, seen):
        su, sv, st = source_of(s)
        distance = lax.rem(sv - v + RING, RING)
        for a in range(AB):
            seen = jnp.where(code == distance * TILE + su * MINE + a * HELD + st, 1.0, seen)
        return seen

    need_tx[...] = lax.fori_loop(0, NS, mark, jnp.zeros((RING, 8, TILE), jnp.float32))

    pool[plan.zero_slot] = jnp.zeros((TILE, TILE), jnp.bfloat16)

    for copy in load_copies:
        copy.wait()
    pl.semaphore_wait(barrier, 3 * (RING - 1))

    def remote(src, dst, send, recv, there):
        return pltpu.make_async_remote_copy(
            src_ref=src, dst_ref=dst, send_sem=send, recv_sem=recv, device_id=there, device_id_type=MESH
        )

    def first(sign, hop, block, arrival=False):
        behind = lax.rem(u + (hop - 1 + arrival if sign else RING - hop + 1 - arrival), RING)
        ref = group.at[pl.ds(behind * MINE + block, 1)]
        number = (sign * HOPS + hop - 1) * MINE + block
        return remote(ref, ref, one_send.at[number], one_recv.at[number], on_first(-1 if sign else 1))

    def first_wait(sign, hop, block):
        first(sign, hop, block, arrival=True).wait_recv()

    need_copies = [
        remote(need_tx.at[j], need_rx.at[j], need_send.at[j], need_recv.at[j], on_second(j)) for j in range(1, RING)
    ]
    mask_copies = [
        remote(mask_rx.at[0], mask_rx.at[j], mask_send.at[j], mask_recv.at[j], on_first(j)) for j in range(1, RING)
    ]
    sent = []

    def start(copy):
        copy.start()
        sent.append(copy)

    for block in range(MINE):
        for sign in range(2):
            start(first(sign, 1, block))
        if block == 1:
            for copy in need_copies + mask_copies:
                start(copy)

    def forward(hop):
        for block in range(MINE):
            for sign in range(2):
                first_wait(sign, hop - 1, block)
                start(first(sign, hop, block))

    forward(2)

    for copy in need_copies + mask_copies:
        copy.wait_recv()
    mask = mask_rx[0]
    for j in range(1, RING):
        mask = jnp.maximum(mask, mask_rx[j])
    even = (lane % 2) == 0
    flane = lane.astype(jnp.float32)
    wide_lane = lax.broadcasted_iota(jnp.int32, (GROUP, TILE), 1)
    wide_row = lax.broadcasted_iota(jnp.int32, (GROUP, TILE), 0)
    far = []
    for sign in range(2):
        reach = jnp.zeros((8, TILE), jnp.float32)
        for distance in range(1, HOPS):
            needed = need_rx[distance if sign else RING - distance] * mask
            reach = jnp.where(needed > 0.0, float(distance), reach)
        far.append(reach)
    opposite = need_rx[HOPS] * mask > 0.0
    far[0] = jnp.where(jnp.logical_and(opposite, even), float(HOPS), far[0])
    far[1] = jnp.where(jnp.logical_and(opposite, jnp.logical_not(even)), float(HOPS), far[1])
    ranks = []
    over = jnp.zeros((8, TILE), jnp.float32)
    for sign in range(2):
        for hop in range(1, HOPS + 1):
            count = jnp.sum(jnp.where(far[sign] >= float(hop), 1.0, 0.0), axis=1, keepdims=True)
            over = jnp.maximum(over, jnp.where(count > float(plan.caps[hop - 1]), 1.0, 0.0))
        key = far[sign] * float(TILE) + (float(TILE - 1) - flane)
        key_row = jnp.broadcast_to(key[0:1], (GROUP, TILE))
        key_col = jnp.sum(jnp.where(wide_lane == wide_row, key_row, 0.0), axis=1, keepdims=True)
        rank_row = jnp.sum(jnp.where(key_col > key_row, 1.0, 0.0), axis=0, keepdims=True)
        rank_col = jnp.sum(jnp.where(key_row > key_col, 1.0, 0.0), axis=1, keepdims=True)
        chosen = jnp.where(rank_col == wide_lane.astype(jnp.float32), wide_row.astype(jnp.float32), 0.0)
        inverse = jnp.sum(chosen, axis=0, keepdims=True)
        order[sign] = jnp.broadcast_to(inverse, (8, TILE)).astype(jnp.int32)
        ranks.append(jnp.broadcast_to(rank_row, (8, TILE)))
    order_copy = pltpu.make_async_copy(order, order_s, local_sem.at[1])
    order_copy.start()
    forward(3)

    sub = lax.broadcasted_iota(jnp.int32, (8, TILE), 0)
    for j in range(1, RING):
        right = ranks[0] + float(plan.region(0, min(j, HOPS)))
        left = ranks[1] + float(plan.region(1, min(RING - j, HOPS)))
        slot = right if j < HOPS else left if j > HOPS else jnp.where(even, right, left)
        slot = jnp.where(mask > 0.0, slot, float(plan.zero_slot))
        tab_tx[j] = jnp.where(sub == 0, slot, over).astype(jnp.int32)
    tab_copies = [
        remote(tab_tx.at[j], tab_rx.at[j], tab_send.at[j], tab_recv.at[j], on_second(j)) for j in range(1, RING)
    ]
    tab_rx[0] = jnp.where(sub == 0, jnp.where(mask > 0.0, flane, float(plan.zero_slot)), over).astype(jnp.int32)

    for copy in tab_copies:
        start(copy)

    for block in range(MINE):
        for sign in range(2):
            first_wait(sign, HOPS - 1, block)
            if block % 2 == sign:
                start(first(sign, HOPS, block))
    order_copy.wait()
    for block in range(MINE):
        first_wait(block % 2, HOPS, block)

    def second(sign, hop, piece):
        begin, size, _ = plan.pieces[piece]
        if hop == 1:
            src = lists.at[sign, pl.ds(begin, size)]
        else:
            src = pool.at[pl.ds(plan.region(sign, hop - 1) + begin, size)]
        dst = pool.at[pl.ds(plan.region(sign, hop) + begin, size)]
        number = (sign * HOPS + hop - 1) * len(plan.pieces) + piece
        return remote(src, dst, two_send.at[number], two_recv.at[number], on_second(-1 if sign else 1))

    for piece, (begin, size, _) in enumerate(plan.pieces):
        for sign in range(2):
            for r in range(begin, begin + size):
                lists[sign, r] = group[jnp.clip(order_s[sign, 0, r], 0, GROUP - 1)]
            start(second(sign, 1, piece))
    own_copy = pltpu.make_async_copy(group, pool.at[pl.ds(0, GROUP)], local_sem.at[2])
    own_copy.start()

    for copy in tab_copies:
        copy.wait_recv()
    tab_copy = pltpu.make_async_copy(tab_rx, tab_s, local_sem.at[3])
    tab_copy.start()
    vote = tab_rx[0]
    for j in range(1, RING):
        vote = jnp.maximum(vote, tab_rx[j])
    vote_tx[...] = jnp.broadcast_to(vote[1:2], (8, TILE))
    vote_copies = [
        remote(vote_tx, vote_rx.at[j], vote_send.at[j], vote_recv.at[j], on_first(j)) for j in range(1, RING)
    ]
    for copy in vote_copies:
        start(copy)

    tab_copy.wait()

    def locate(s, carry):
        su, sv, st = source_of(s)
        distance = lax.rem(v - sv + RING, RING)
        for a in range(AB):
            slot = tab_s[distance, 0, su * MINE + a * HELD + st]
            index_s[s * AB + a] = jnp.clip(slot, 0, plan.zero_slot)
        return carry

    lax.fori_loop(0, NS, locate, 0)

    for hop in range(2, HOPS + 1):
        for piece, (_, _, hops) in enumerate(plan.pieces):
            if hops >= hop:
                for sign in range(2):
                    second(sign, hop - 1, piece).wait_recv()
                    start(second(sign, hop, piece))
    for copy in vote_copies:
        copy.wait_recv()
    vote = vote_tx[...]
    for j in range(1, RING):
        vote = jnp.maximum(vote, vote_rx[j])
    vote_wide = jnp.concatenate([vote, vote], axis=1).astype(jnp.float32)
    own_copy.wait()
    amp_copy.wait()
    for piece, (_, _, hops) in enumerate(plan.pieces):
        for sign in range(2):
            second(sign, hops, piece).wait_recv()

    total[...] = jnp.zeros_like(total)

    def multiply(i, carry):
        tiles = [amp[STEP * i + j] for j in range(STEP)]
        bands = [
            jnp.concatenate([pool[index_s[(STEP * i + j) * AB + a]] for j in range(STEP)], axis=0) for a in range(AB)
        ]
        total[...] += jnp.dot(
            jnp.concatenate(tiles, axis=1), jnp.concatenate(bands, axis=1), preferred_element_type=jnp.float32
        )
        return carry

    lax.fori_loop(0, NS // STEP, multiply, 0)

    for q in range(KA):
        part_tx[q, 0:ROWS] = total[q * ROWS : (q + 1) * ROWS]
        part_tx[q, ROWS : ROWS + 8] = vote_wide
    part_copies = [
        remote(part_tx.at[lax.rem(ka + j, KA)], part_rx.at[j], part_send.at[j], part_recv.at[j], on_ka(j))
        for j in range(1, KA)
    ]
    for copy in part_copies:
        copy.start()
    for copy in sent:
        copy.wait_send()
    result = part_tx[ka, 0:ROWS]
    for copy in part_copies:
        copy.wait_recv()
    vote = vote_wide
    for j in range(1, KA):
        result += part_rx[j, 0:ROWS]
        vote = jnp.maximum(vote, part_rx[j, ROWS : ROWS + 8])
    out_ref[...] = result
    flag_ref[0] = jnp.max(vote).astype(jnp.int32)
    for copy in part_copies:
        copy.wait_send()


def ladder(plan, number, amplitude, slot_owner, slot_tile, integrals, tile_mask):
    scratch = [
        pltpu.VMEM((NS, TILE, TILE), jnp.bfloat16),
        pltpu.VMEM((GROUP, TILE, TILE), jnp.bfloat16),
        pltpu.VMEM((2, plan.caps[0], TILE, TILE), jnp.bfloat16),
        pltpu.VMEM((plan.slots, TILE, TILE), jnp.bfloat16),
        pltpu.VMEM((RING, 8, TILE), jnp.float32),
        pltpu.VMEM((RING, 8, TILE), jnp.float32),
        pltpu.VMEM((RING, 8, TILE), jnp.float32),
        pltpu.VMEM((2, 8, TILE), jnp.int32),
        pltpu.VMEM((RING, 8, TILE), jnp.int32),
        pltpu.VMEM((RING, 8, TILE), jnp.int32),
        pltpu.VMEM((8, TILE), jnp.int32),
        pltpu.VMEM((RING, 8, TILE), jnp.int32),
        pltpu.SMEM((2, 8, TILE), jnp.int32),
        pltpu.SMEM((RING, 8, TILE), jnp.int32),
        pltpu.SMEM((NS * AB,), jnp.int32),
        pltpu.VMEM((TILE, AB * TILE), jnp.float32),
        pltpu.VMEM((KA, ROWS + 8, AB * TILE), jnp.float32),
        pltpu.VMEM((KA, ROWS + 8, AB * TILE), jnp.float32),
        pltpu.SemaphoreType.DMA((6,)),
        pltpu.SemaphoreType.DMA((2 * HOPS * MINE,)),
        pltpu.SemaphoreType.DMA((2 * HOPS * MINE,)),
        pltpu.SemaphoreType.DMA((2 * HOPS * len(plan.pieces),)),
        pltpu.SemaphoreType.DMA((2 * HOPS * len(plan.pieces),)),
    ] + [pltpu.SemaphoreType.DMA((RING,)) for _ in range(10)]
    smem, vmem = pl.BlockSpec(memory_space=pltpu.SMEM), pl.BlockSpec(memory_space=pltpu.VMEM)
    hbm = pl.BlockSpec(memory_space=pl.ANY)
    return pl.pallas_call(
        functools.partial(kernel, plan),
        out_shape=(
            jax.ShapeDtypeStruct((ROWS, AB * TILE), jnp.float32),
            jax.ShapeDtypeStruct((1,), jnp.int32),
        ),
        in_specs=[smem, smem, vmem, hbm, hbm],
        out_specs=(vmem, smem),
        scratch_shapes=scratch,
        compiler_params=pltpu.CompilerParams(
            collective_id=number, has_side_effects=True, vmem_limit_bytes=32 * 1024 * 1024
        ),
    )(slot_owner, slot_tile, tile_mask.T, integrals, amplitude)


def local(*arrays):
    result, over = ladder(Plan(USUAL), 0, *arrays)
    return lax.cond(over[0] > 0, lambda: ladder(Plan(EVERY), 1, *arrays)[0], lambda: result)


def solution(mesh):
    in_specs = (
        P(("pair", "ka"), None, None),
        P(("pair", "ka")),
        P(("pair", "ka")),
        P(("pair", "ka"), None, None),
        P(("pair", "ka"), None),
    )
    out_specs = P(("pair", "ka"), None)
    return jax.shard_map(local, mesh=mesh, in_specs=in_specs, out_specs=out_specs, check_vma=False)
```

```python
import functools

import jax
import jax.numpy as jnp
from jax import lax
from jax.experimental import pallas as pl
from jax.experimental.pallas import tpu as pltpu
from jax.sharding import PartitionSpec as P

MESH = pl.DeviceIdType.MESH

TILE = 128
AB = 2
HELD = 3
NS = 48
RING = 8
KA = 8
MINE = HELD * AB
GROUP = RING * MINE
CHUNK = 1
STEP = 8
ROWS = TILE // KA

HOPS = RING // 2
LONGEST = 6


class Plan:
    def __init__(self, sizes, spare):
        self.sizes, self.spare = sizes, spare
        self.zero_slot = GROUP + 2 * sum(sizes)
        self.slots = self.zero_slot + 1
        self.held = sizes[0] + spare[1]
        self.pieces = {1: self.cut(0, sizes[0], "own")}
        self.staged = {}
        self.stage = 0
        for phase in range(2, HOPS + 1):
            size = sizes[phase - 1]
            mixed, back = size - spare[phase - 1], min(size, sizes[0])
            front = self.cut(0, mixed, "front") + self.cut(mixed, back, "mixed")
            rear = self.cut(back, size, "back")
            self.pieces[phase] = rear + front if phase == 2 else front + rear
            self.staged[phase] = self.stage - mixed
            self.stage += back - mixed

    @staticmethod
    def cut(begin, end, kind):
        count = -(-(end - begin) // LONGEST)
        edges = [begin + (end - begin) * i // count for i in range(count + 1)] if count else []
        return [(a, b, kind) for a, b in zip(edges, edges[1:])]

    def region(self, sign, phase):
        return GROUP + sign * sum(self.sizes) + sum(self.sizes[: phase - 1])


USUAL = Plan((22, 24, 22, 12), (0, 12, 9, 6))
EVERY = Plan((GROUP, GROUP, GROUP, GROUP // 2), (0, 0, 0, 0))


def kernel(
    plan, owner_ref, tile_ref, owner_row, tile_row, mask_ref, integrals_ref, amplitude_ref,
    out_ref, flag_ref,
    amp, group, lists, stage, pool, need_tx, need_rx, mask_rx, order, tab_tx, tab_rx, near_tx, near_rx, vote_tx, vote_rx, last_tx, last_rx,
    order_s, tab_s, index_s, total, part_rx,
    local_sem, one_send, one_recv, two_send, two_recv, need_send, need_recv, mask_send, mask_recv,
    tab_send, tab_recv, near_send, near_recv, vote_send, vote_recv, last_send, last_recv, part_send, part_recv,
):
    pair, ka = lax.axis_index("pair"), lax.axis_index("ka")
    core = lax.rem(ka, 2)
    high, low = lax.div(pair, RING), lax.rem(pair, RING)
    u = high + core * (low - high)
    v = low + core * (high - low)
    stride_u, stride_v = RING - (RING - 1) * core, 1 + (RING - 1) * core

    def on_first(step):
        return (lax.rem(u + step + RING, RING) * stride_u + v * stride_v, ka)

    def on_second(step):
        return (u * stride_u + lax.rem(v + step + RING, RING) * stride_v, ka)

    def on_ka(step):
        return (pair, lax.rem(ka + step, KA))

    load_copies = [
        pltpu.make_async_copy(
            integrals_ref.at[:, :, pl.ds(a * TILE, TILE)],
            group.at[pl.ds(u * MINE + a * HELD, HELD)],
            local_sem.at[4 + a],
        )
        for a in range(AB)
    ]
    for copy in load_copies:
        copy.start()

    barrier = pltpu.get_barrier_semaphore()
    for step in range(1, RING):
        for there in (on_first(step), on_second(step), on_ka(step)):
            pl.semaphore_signal(barrier, inc=1, device_id=there, device_id_type=MESH)

    amp_copy = pltpu.make_async_copy(amplitude_ref, amp, local_sem.at[0])

    lane = lax.broadcasted_iota(jnp.int32, (8, TILE), 1)
    own_mask = jnp.zeros((8, TILE), jnp.float32)
    for t in range(HELD):
        for a in range(AB):
            here = lane == u * MINE + a * HELD + t
            own_mask = jnp.where(here, mask_ref[a : a + 1, t : t + 1].astype(jnp.float32), own_mask)
    mask_rx[0] = own_mask

    def source_of(s):
        owner = owner_ref[s]
        oh, ol = lax.div(owner, RING), lax.rem(owner, RING)
        return oh + core * (ol - oh), ol + core * (oh - ol), tile_ref[s]

    slot_lane = lax.broadcasted_iota(jnp.int32, (NS, NS), 1)
    slot_row = lax.broadcasted_iota(jnp.int32, (NS, NS), 0)
    owner_high, owner_low = lax.shift_right_logical(owner_row[...], 3), lax.bitwise_and(owner_row[...], RING - 1)
    owner_u = owner_high + core * (owner_low - owner_high)
    owner_v = owner_low + core * (owner_high - owner_low)
    steps = lax.bitwise_and(owner_v - v, RING - 1)
    target = (steps * TILE + owner_u * MINE + tile_row[...]).astype(jnp.float32)
    target = jnp.sum(jnp.where(slot_lane == slot_row, jnp.broadcast_to(target, (NS, NS)), 0.0), axis=1, keepdims=True)
    ahead = target - lax.broadcasted_iota(jnp.int32, (NS, TILE), 1).astype(jnp.float32)
    for j in range(RING):
        used = jnp.zeros((NS, TILE), jnp.float32)
        for a in range(AB):
            used = jnp.where(ahead == float(j * TILE - a * HELD), 1.0, used)
        need_tx[j] = jnp.broadcast_to(jnp.max(used, axis=0, keepdims=True), (8, TILE))

    pool[plan.zero_slot] = jnp.zeros((TILE, TILE), jnp.bfloat16)

    for copy in load_copies:
        copy.wait()
    pl.semaphore_wait(barrier, 3 * (RING - 1))

    def remote(src, dst, send, recv, there):
        return pltpu.make_async_remote_copy(
            src_ref=src, dst_ref=dst, send_sem=send, recv_sem=recv, device_id=there, device_id_type=MESH
        )

    def first(sign, hop, block, arrival=False):
        behind = lax.rem(u + (hop - 1 + arrival if sign else RING - hop + 1 - arrival), RING)
        ref = group.at[pl.ds(behind * MINE + block, CHUNK)]
        number = (sign * HOPS + hop - 1) * MINE + block
        return remote(ref, ref, one_send.at[number], one_recv.at[number], on_first(-1 if sign else 1))

    def first_wait(sign, hop, block):
        first(sign, hop, block, arrival=True).wait_recv()

    need_copies = [
        remote(need_tx.at[j], need_rx.at[j], need_send.at[j], need_recv.at[j], on_second(j)) for j in range(1, RING)
    ]
    mask_copies = [
        remote(mask_rx.at[0], mask_rx.at[j], mask_send.at[j], mask_recv.at[j], on_first(j)) for j in range(1, RING)
    ]
    sent = []

    def start(copy):
        copy.start()
        sent.append(copy)

    for block in range(0, MINE, CHUNK):
        for sign in range(2):
            start(first(sign, 1, block))
        if block == 0:
            for copy in need_copies + mask_copies:
                start(copy)
    amp_copy.start()

    def forward(hop):
        for block in range(0, MINE, CHUNK):
            for sign in range(2):
                first_wait(sign, hop - 1, block)
                start(first(sign, hop, block))

    forward(2)

    for copy in need_copies + mask_copies:
        copy.wait_recv()
    mask = mask_rx[0]
    for j in range(1, RING):
        mask = jnp.maximum(mask, mask_rx[j])
    even = (lane % 2) == 0
    flane = lane.astype(jnp.float32)
    wide_lane = lax.broadcasted_iota(jnp.int32, (GROUP, TILE), 1)
    wide_row = lax.broadcasted_iota(jnp.int32, (GROUP, TILE), 0)
    far = []
    for sign in range(2):
        reach = jnp.zeros((8, TILE), jnp.float32)
        for distance in range(1, HOPS):
            needed = need_rx[distance if sign else RING - distance] * mask
            reach = jnp.where(needed > 0.0, float(distance), reach)
        far.append(reach)
    opposite = need_rx[HOPS] * mask > 0.0
    far[0] = jnp.where(jnp.logical_and(opposite, even), float(HOPS), far[0])
    far[1] = jnp.where(jnp.logical_and(opposite, jnp.logical_not(even)), float(HOPS), far[1])
    ranks = []
    counts = []
    for sign in range(2):
        counts.append(
            [
                jnp.broadcast_to(
                    jnp.sum(jnp.where(far[sign] >= float(hop), 1.0, 0.0), axis=1, keepdims=True), (8, TILE)
                )
                for hop in range(1, HOPS + 1)
            ]
        )
        key = far[sign] * float(TILE) + (float(TILE - 1) - flane)
        key_row = jnp.broadcast_to(key[0:1], (GROUP, TILE))
        key_col = jnp.sum(jnp.where(wide_lane == wide_row, key_row, 0.0), axis=1, keepdims=True)
        rank_row = jnp.sum(jnp.where(key_col > key_row, 1.0, 0.0), axis=0, keepdims=True)
        rank_col = jnp.sum(jnp.where(key_row > key_col, 1.0, 0.0), axis=1, keepdims=True)
        chosen = jnp.where(rank_col == wide_lane.astype(jnp.float32), wide_row.astype(jnp.float32), 0.0)
        inverse = jnp.sum(chosen, axis=0, keepdims=True)
        order[sign] = jnp.broadcast_to(inverse, (8, TILE)).astype(jnp.int32)
        ranks.append(jnp.broadcast_to(rank_row, (8, TILE)))
    order_copy = pltpu.make_async_copy(order, order_s, local_sem.at[1])
    order_copy.start()
    forward(3)

    sub = lax.broadcasted_iota(jnp.int32, (8, TILE), 0)
    kept = float(plan.sizes[0])

    def slot_of(sign, hops):
        slot = ranks[sign] + float(plan.region(sign, hops))
        if hops < HOPS and plan.spare[hops]:
            last = plan.region(sign, hops + 1) + plan.sizes[hops] - 1
            slot = jnp.where(ranks[sign] >= kept, float(last) + kept - ranks[sign], slot)
        return slot

    rows = jnp.zeros((8, TILE), jnp.float32)
    for sign in range(2):
        for hop in range(2, HOPS + 1):
            rows = jnp.where(sub == sign * (HOPS - 1) + hop - 1, counts[sign][hop - 1], rows)
    for j in range(1, RING):
        if j == HOPS:
            slot = jnp.where(even, slot_of(0, HOPS), slot_of(1, HOPS))
        else:
            slot = slot_of(0, j) if j < HOPS else slot_of(1, RING - j)
        slot = jnp.where(mask > 0.0, slot, float(plan.zero_slot))
        tab_tx[j] = jnp.where(sub == 0, slot, rows).astype(jnp.int32)
    tab_copies = [
        remote(tab_tx.at[j], tab_rx.at[j], tab_send.at[j], tab_recv.at[j], on_second(j)) for j in range(1, RING)
    ]
    tab_rx[0] = jnp.where(mask > 0.0, flane, float(plan.zero_slot)).astype(jnp.int32)

    for copy in tab_copies:
        start(copy)

    for block in range(0, MINE, CHUNK):
        for sign in range(2):
            first_wait(sign, HOPS - 1, block)
            if block * 2 // MINE == sign:
                start(first(sign, HOPS, block))
    order_copy.wait()
    for block in range(0, MINE, CHUNK):
        first_wait(block * 2 // MINE, HOPS, block)

    early = len(sent)

    numbers = {}
    for sign in range(2):
        for phase, pieces in plan.pieces.items():
            for piece in pieces:
                numbers[sign, phase, piece] = len(numbers)

    def second(sign, phase, piece):
        begin, end, kind = piece
        size = end - begin
        if kind == "own":
            src = lists.at[sign, pl.ds(begin, size)]
        elif kind == "front":
            src = pool.at[pl.ds(plan.region(sign, phase - 1) + begin, size)]
        elif kind == "mixed":
            src = stage.at[sign, pl.ds(plan.staged[phase] + begin, size)]
        elif phase == 2:
            src = lists.at[sign, pl.ds(plan.held - plan.sizes[1] + begin, size)]
        else:
            shift = plan.sizes[phase - 2] - plan.sizes[phase - 1]
            src = pool.at[pl.ds(plan.region(sign, phase - 1) + shift + begin, size)]
        number = numbers[sign, phase, piece]
        dst = pool.at[pl.ds(plan.region(sign, phase) + begin, size)]
        return remote(src, dst, two_send.at[number], two_recv.at[number], on_second(-1 if sign else 1))

    arrived = set()

    def await_slots(sign, phase, begin, end):
        for piece in plan.pieces[phase]:
            if piece[0] < end and begin < piece[1] and (sign, phase, piece) not in arrived:
                arrived.add((sign, phase, piece))
                second(sign, phase, piece).wait_recv()

    def pick(sign, place, rank):
        lists[sign, place] = group[jnp.clip(order_s[sign, 0, rank], 0, GROUP - 1)]

    for piece in plan.pieces[1]:
        for sign in range(2):
            for rank in range(piece[0], piece[1]):
                pick(sign, rank, rank)
            start(second(sign, 1, piece))
    for sign in range(2):
        for i in range(plan.spare[1]):
            pick(sign, plan.held - 1 - i, plan.sizes[0] + i)
    for piece in plan.pieces[2]:
        if piece[2] == "back":
            for sign in range(2):
                start(second(sign, 2, piece))
    own_copy = pltpu.make_async_copy(group, pool.at[pl.ds(0, GROUP)], local_sem.at[2])
    own_copy.start()

    for copy in tab_copies:
        copy.wait_recv()
    tab_copy = pltpu.make_async_copy(tab_rx, tab_s, local_sem.at[3])
    tab_copy.start()

    over = jnp.zeros((8, TILE), jnp.float32)
    left_over = {}
    for sign in range(2):
        moving = [counts[sign][0]]
        for behind in range(1, HOPS):
            table = tab_rx[RING - behind if sign else behind].astype(jnp.float32)
            for hop in (behind, behind + 1):
                if hop > 1:
                    row = sign * (HOPS - 1) + hop - 1
                    moving.append(jnp.broadcast_to(table[row : row + 1], (8, TILE)))
        passed = {2: moving[1], 3: moving[3], 4: moving[5]}
        came = {2: moving[0], 3: moving[1], 4: moving[3]}
        over = jnp.maximum(over, jnp.where(passed[HOPS] > kept, 1.0, 0.0))
        for phase in range(2, HOPS + 1):
            rest = jnp.maximum(came[phase] - kept, 0.0)
            front = jnp.minimum(passed[phase], kept)
            over = jnp.maximum(over, jnp.where(rest > float(plan.spare[phase - 1]), 1.0, 0.0))
            over = jnp.maximum(over, jnp.where(rest + front > float(plan.sizes[phase - 1]), 1.0, 0.0))
            left_over[sign, phase] = rest

    def spread(vote, tx, rx, send, recv, there):
        tx[...] = vote
        copies = [remote(tx, rx.at[j], send.at[j], recv.at[j], there(j)) for j in range(1, RING)]
        for copy in copies:
            start(copy)
        return copies

    def collect(copies, tx, rx):
        for copy in copies:
            copy.wait_recv()
        vote = tx[...]
        for j in range(1, RING):
            vote = jnp.maximum(vote, rx[j])
        return vote

    near_copies = spread(over, near_tx, near_rx, near_send, near_recv, on_second)

    tab_copy.wait()

    def locate(s, carry):
        su, sv, st = source_of(s)
        distance = lax.rem(v - sv + RING, RING)
        for a in range(AB):
            slot = tab_s[distance, 0, su * MINE + a * HELD + st]
            index_s[s * AB + a] = jnp.clip(slot, 0, plan.zero_slot)
        return carry

    lax.fori_loop(0, NS, locate, 0)

    for copy in sent[:early]:
        copy.wait_send()
    del sent[:early]
    for phase in range(2, HOPS + 1):
        size, shift = plan.sizes[phase - 1], plan.sizes[phase - 2] - plan.sizes[phase - 1]
        behind = len(sent)
        for piece in plan.pieces[phase]:
            begin, end, kind = piece
            if phase == 2 and kind == "back":
                continue
            for sign in range(2):
                before = plan.region(sign, phase - 1)
                if kind == "back":
                    await_slots(sign, phase - 1, begin + shift, end + shift)
                else:
                    await_slots(sign, phase - 1, begin, end)
                if kind == "mixed":
                    if phase > 2:
                        await_slots(sign, phase - 1, begin + shift, end + shift)
                    for slot in range(begin, end):
                        if phase > 2:
                            other = pool[before + slot + shift]
                        else:
                            other = lists[sign, plan.held - size + slot]
                        rest = jnp.broadcast_to(left_over[sign, phase][0:1], (TILE, TILE))
                        chosen = jnp.where(
                            rest > float(size - 1 - slot), other.astype(jnp.float32), pool[before + slot].astype(jnp.float32)
                        )
                        stage[sign, plan.staged[phase] + slot] = chosen.astype(jnp.bfloat16)
                start(second(sign, phase, piece))
        if phase == 2:
            vote = collect(near_copies, near_tx, near_rx)
            vote_copies = spread(vote, vote_tx, vote_rx, vote_send, vote_recv, on_first)
        elif phase == 3:
            vote = collect(vote_copies, vote_tx, vote_rx)
            last_copies = spread(vote, last_tx, last_rx, last_send, last_recv, on_ka)
    flag_ref[0] = jnp.max(collect(last_copies, last_tx, last_rx)).astype(jnp.int32)
    for copy in sent[:behind]:
        copy.wait_send()
    del sent[:behind]
    own_copy.wait()
    amp_copy.wait()
    for phase in range(1, HOPS + 1):
        for sign in range(2):
            await_slots(sign, phase, 0, plan.sizes[phase - 1])

    total[...] = jnp.zeros_like(total)

    def multiply(i, carry):
        tiles = [amp[STEP * i + j] for j in range(STEP)]
        bands = [
            jnp.concatenate([pool[index_s[(STEP * i + j) * AB + a]] for j in range(STEP)], axis=0) for a in range(AB)
        ]
        total[...] += jnp.dot(
            jnp.concatenate(tiles, axis=1), jnp.concatenate(bands, axis=1), preferred_element_type=jnp.float32
        )
        return carry

    lax.fori_loop(0, NS // STEP, multiply, 0)

    part_copies = [
        remote(
            total.at[pl.ds(lax.rem(ka + j, KA) * ROWS, ROWS)], part_rx.at[j], part_send.at[j], part_recv.at[j], on_ka(j)
        )
        for j in range(1, KA)
    ]
    for copy in part_copies:
        copy.start()
    for copy in sent:
        copy.wait_send()
    result = total[pl.ds(pl.multiple_of(ka * ROWS, ROWS), ROWS)]
    for j, copy in enumerate(part_copies, 1):
        copy.wait_recv()
        result += part_rx[j]
    out_ref[...] = result
    for copy in part_copies:
        copy.wait_send()


def ladder(plan, number, amplitude, slot_owner, slot_tile, integrals, tile_mask):
    copies = 2 * sum(len(pieces) for pieces in plan.pieces.values())
    scratch = [
        pltpu.VMEM((NS, TILE, TILE), jnp.bfloat16),
        pltpu.VMEM((GROUP, TILE, TILE), jnp.bfloat16),
        pltpu.VMEM((2, plan.held, TILE, TILE), jnp.bfloat16),
        pltpu.VMEM((2, max(plan.stage, 1), TILE, TILE), jnp.bfloat16),
        pltpu.VMEM((plan.slots, TILE, TILE), jnp.bfloat16),
        pltpu.VMEM((RING, 8, TILE), jnp.float32),
        pltpu.VMEM((RING, 8, TILE), jnp.float32),
        pltpu.VMEM((RING, 8, TILE), jnp.float32),
        pltpu.VMEM((2, 8, TILE), jnp.int32),
        pltpu.VMEM((RING, 8, TILE), jnp.int32),
        pltpu.VMEM((RING, 8, TILE), jnp.int32),
        pltpu.VMEM((8, TILE), jnp.float32),
        pltpu.VMEM((RING, 8, TILE), jnp.float32),
        pltpu.VMEM((8, TILE), jnp.float32),
        pltpu.VMEM((RING, 8, TILE), jnp.float32),
        pltpu.VMEM((8, TILE), jnp.float32),
        pltpu.VMEM((KA, 8, TILE), jnp.float32),
        pltpu.SMEM((2, 8, TILE), jnp.int32),
        pltpu.SMEM((RING, 8, TILE), jnp.int32),
        pltpu.SMEM((NS * AB,), jnp.int32),
        pltpu.VMEM((TILE, AB * TILE), jnp.float32),
        pltpu.VMEM((KA, ROWS, AB * TILE), jnp.float32),
        pltpu.SemaphoreType.DMA((6,)),
        pltpu.SemaphoreType.DMA((2 * HOPS * MINE,)),
        pltpu.SemaphoreType.DMA((2 * HOPS * MINE,)),
        pltpu.SemaphoreType.DMA((copies,)),
        pltpu.SemaphoreType.DMA((copies,)),
    ] + [pltpu.SemaphoreType.DMA((RING,)) for _ in range(14)]
    smem, vmem = pl.BlockSpec(memory_space=pltpu.SMEM), pl.BlockSpec(memory_space=pltpu.VMEM)
    hbm = pl.BlockSpec(memory_space=pl.ANY)
    return pl.pallas_call(
        functools.partial(kernel, plan),
        out_shape=(
            jax.ShapeDtypeStruct((ROWS, AB * TILE), jnp.float32),
            jax.ShapeDtypeStruct((1,), jnp.int32),
        ),
        in_specs=[smem, smem, vmem, vmem, vmem, hbm, hbm],
        out_specs=(vmem, smem),
        scratch_shapes=scratch,
        compiler_params=pltpu.CompilerParams(
            collective_id=number, has_side_effects=True, vmem_limit_bytes=32 * 1024 * 1024
        ),
    )(slot_owner, slot_tile, slot_owner[None], slot_tile[None], tile_mask.T, integrals, amplitude)


def local(*arrays):
    result, over = ladder(USUAL, 0, *arrays)
    return lax.cond(over[0] > 0, lambda: ladder(EVERY, 1, *arrays)[0], lambda: result)


def solution(mesh):
    in_specs = (
        P(("pair", "ka"), None, None),
        P(("pair", "ka")),
        P(("pair", "ka")),
        P(("pair", "ka"), None, None),
        P(("pair", "ka"), None),
    )
    out_specs = P(("pair", "ka"), None)
    return jax.shard_map(local, mesh=mesh, in_specs=in_specs, out_specs=out_specs, check_vma=False)
```

```python
import functools

import jax
import jax.numpy as jnp
from jax import lax
from jax.experimental import pallas as pl
from jax.experimental.pallas import tpu as pltpu
from jax.sharding import PartitionSpec as P

MESH = pl.DeviceIdType.MESH

TILE = 128
AB = 2
HELD = 3
NS = 48
RING = 8
KA = 8
MINE = HELD * AB
GROUP = RING * MINE
CHUNK = 1
STEP = 8
ROWS = TILE // KA

HOPS = RING // 2
LONGEST = 4


class Plan:
    def __init__(self, sizes, spare):
        self.sizes, self.spare = sizes, spare
        self.zero_slot = GROUP + 2 * sum(sizes)
        self.slots = self.zero_slot + 1
        self.held = sizes[0] + spare[1]
        self.pieces = {1: self.cut(0, sizes[0], "own")}
        self.staged = {}
        self.stage = 0
        for phase in range(2, HOPS + 1):
            size = sizes[phase - 1]
            mixed, back = size - spare[phase - 1], min(size, sizes[0])
            front = self.cut(0, mixed, "front") + self.cut(mixed, back, "mixed")
            rear = self.cut(back, size, "back")
            self.pieces[phase] = rear + front if phase == 2 else front + rear
            self.staged[phase] = self.stage - mixed
            self.stage += back - mixed

    @staticmethod
    def cut(begin, end, kind):
        count = -(-(end - begin) // LONGEST)
        edges = [begin + (end - begin) * i // count for i in range(count + 1)] if count else []
        return [(a, b, kind) for a, b in zip(edges, edges[1:])]

    def region(self, sign, phase):
        return GROUP + sign * sum(self.sizes) + sum(self.sizes[: phase - 1])


USUAL = Plan((22, 24, 22, 12), (0, 12, 9, 6))
EVERY = Plan((GROUP, GROUP, GROUP, GROUP // 2), (0, 0, 0, 0))


def kernel(
    plan, owner_hbm, tile_hbm, owner_row_hbm, tile_row_hbm, mask_hbm, integrals_ref, amplitude_ref,
    out_ref, flag_ref,
    owner_ref, tile_ref, owner_row, tile_row, mask_ref, amp, group, lists, stage, pool, need_tx, need_rx, mask_rx, order, tab_tx, tab_rx, near_tx, near_rx, vote_tx, vote_rx, last_tx, last_rx,
    order_s, tab_s, index_s, total, part_rx,
    local_sem, one_send, one_recv, two_send, two_recv, need_send, need_recv, mask_send, mask_recv,
    tab_send, tab_recv, near_send, near_recv, vote_send, vote_recv, last_send, last_recv, part_send, part_recv,
):
    pair, ka = lax.axis_index("pair"), lax.axis_index("ka")
    core = lax.rem(ka, 2)
    high, low = lax.div(pair, RING), lax.rem(pair, RING)
    u = high + core * (low - high)
    v = low + core * (high - low)
    stride_u, stride_v = RING - (RING - 1) * core, 1 + (RING - 1) * core

    def on_first(step):
        return (lax.rem(u + step + RING, RING) * stride_u + v * stride_v, ka)

    def on_second(step):
        return (u * stride_u + lax.rem(v + step + RING, RING) * stride_v, ka)

    def on_ka(step):
        return (pair, lax.rem(ka + step, KA))

    load_copies = [
        pltpu.make_async_copy(
            integrals_ref.at[:, :, pl.ds(a * TILE, TILE)],
            group.at[pl.ds(u * MINE + a * HELD, HELD)],
            local_sem.at[4 + a],
        )
        for a in range(AB)
    ]
    for copy in load_copies:
        copy.start()

    small_copies = [
        pltpu.make_async_copy(source, target, local_sem.at[6 + i])
        for i, (source, target) in enumerate(
            (
                (owner_row_hbm, owner_row),
                (tile_row_hbm, tile_row),
                (mask_hbm, mask_ref),
                (owner_hbm, owner_ref),
                (tile_hbm, tile_ref),
            )
        )
    ]
    for copy in small_copies:
        copy.start()

    barrier = pltpu.get_barrier_semaphore()
    for step in range(1, RING):
        for there in (on_first(step), on_second(step), on_ka(step)):
            pl.semaphore_signal(barrier, inc=1, device_id=there, device_id_type=MESH)

    amp_copy = pltpu.make_async_copy(amplitude_ref, amp, local_sem.at[0])

    for copy in small_copies:
        copy.wait()
    lane = lax.broadcasted_iota(jnp.int32, (8, TILE), 1)
    own_mask = jnp.zeros((8, TILE), jnp.float32)
    for t in range(HELD):
        for a in range(AB):
            here = lane == u * MINE + a * HELD + t
            own_mask = jnp.where(here, mask_ref[a : a + 1, t : t + 1].astype(jnp.float32), own_mask)
    mask_rx[0] = own_mask

    def source_of(s):
        owner = owner_ref[s]
        oh, ol = lax.div(owner, RING), lax.rem(owner, RING)
        return oh + core * (ol - oh), ol + core * (oh - ol), tile_ref[s]

    slot_lane = lax.broadcasted_iota(jnp.int32, (NS, NS), 1)
    slot_row = lax.broadcasted_iota(jnp.int32, (NS, NS), 0)
    owner_high, owner_low = lax.shift_right_logical(owner_row[...], 3), lax.bitwise_and(owner_row[...], RING - 1)
    owner_u = owner_high + core * (owner_low - owner_high)
    owner_v = owner_low + core * (owner_high - owner_low)
    steps = lax.bitwise_and(owner_v - v, RING - 1)
    target = (steps * TILE + owner_u * MINE + tile_row[...]).astype(jnp.float32)
    target = jnp.sum(jnp.where(slot_lane == slot_row, jnp.broadcast_to(target, (NS, NS)), 0.0), axis=1, keepdims=True)
    ahead = target - lax.broadcasted_iota(jnp.int32, (NS, TILE), 1).astype(jnp.float32)
    for j in range(RING):
        used = jnp.zeros((NS, TILE), jnp.float32)
        for a in range(AB):
            used = jnp.where(ahead == float(j * TILE - a * HELD), 1.0, used)
        need_tx[j] = jnp.broadcast_to(jnp.max(used, axis=0, keepdims=True), (8, TILE))

    pool[plan.zero_slot] = jnp.zeros((TILE, TILE), jnp.bfloat16)

    for copy in load_copies:
        copy.wait()
    pl.semaphore_wait(barrier, 3 * (RING - 1))

    def remote(src, dst, send, recv, there):
        return pltpu.make_async_remote_copy(
            src_ref=src, dst_ref=dst, send_sem=send, recv_sem=recv, device_id=there, device_id_type=MESH
        )

    def first(sign, hop, block, arrival=False):
        behind = lax.rem(u + (hop - 1 + arrival if sign else RING - hop + 1 - arrival), RING)
        ref = group.at[pl.ds(behind * MINE + block, CHUNK)]
        number = (sign * HOPS + hop - 1) * MINE + block
        return remote(ref, ref, one_send.at[number], one_recv.at[number], on_first(-1 if sign else 1))

    def first_wait(sign, hop, block):
        first(sign, hop, block, arrival=True).wait_recv()

    need_copies = [
        remote(need_tx.at[j], need_rx.at[j], need_send.at[j], need_recv.at[j], on_second(j)) for j in range(1, RING)
    ]
    mask_copies = [
        remote(mask_rx.at[0], mask_rx.at[j], mask_send.at[j], mask_recv.at[j], on_first(j)) for j in range(1, RING)
    ]
    sent = []

    def start(copy):
        copy.start()
        sent.append(copy)

    for block in range(0, MINE, CHUNK):
        for sign in range(2):
            start(first(sign, 1, block))
        if block == HELD - CHUNK:
            for copy in need_copies + mask_copies:
                start(copy)
    amp_copy.start()

    def forward(hop):
        for block in range(0, MINE, CHUNK):
            for sign in range(2):
                first_wait(sign, hop - 1, block)
                start(first(sign, hop, block))

    forward(2)

    for copy in need_copies + mask_copies:
        copy.wait_recv()
    mask = mask_rx[0]
    for j in range(1, RING):
        mask = jnp.maximum(mask, mask_rx[j])
    even = (lane % 2) == 0
    flane = lane.astype(jnp.float32)
    wide_lane = lax.broadcasted_iota(jnp.int32, (GROUP, TILE), 1)
    wide_row = lax.broadcasted_iota(jnp.int32, (GROUP, TILE), 0)
    far = []
    for sign in range(2):
        reach = jnp.zeros((8, TILE), jnp.float32)
        for distance in range(1, HOPS):
            needed = need_rx[distance if sign else RING - distance] * mask
            reach = jnp.where(needed > 0.0, float(distance), reach)
        far.append(reach)
    opposite = need_rx[HOPS] * mask > 0.0
    far[0] = jnp.where(jnp.logical_and(opposite, even), float(HOPS), far[0])
    far[1] = jnp.where(jnp.logical_and(opposite, jnp.logical_not(even)), float(HOPS), far[1])
    ranks = []
    counts = []
    for sign in range(2):
        counts.append(
            [
                jnp.broadcast_to(
                    jnp.sum(jnp.where(far[sign] >= float(hop), 1.0, 0.0), axis=1, keepdims=True), (8, TILE)
                )
                for hop in range(1, HOPS + 1)
            ]
        )
        key = far[sign] * float(TILE) + (float(TILE - 1) - flane)
        key_row = jnp.broadcast_to(key[0:1], (GROUP, TILE))
        key_col = jnp.sum(jnp.where(wide_lane == wide_row, key_row, 0.0), axis=1, keepdims=True)
        rank_row = jnp.sum(jnp.where(key_col > key_row, 1.0, 0.0), axis=0, keepdims=True)
        rank_col = jnp.sum(jnp.where(key_row > key_col, 1.0, 0.0), axis=1, keepdims=True)
        chosen = jnp.where(rank_col == wide_lane.astype(jnp.float32), wide_row.astype(jnp.float32), 0.0)
        inverse = jnp.sum(chosen, axis=0, keepdims=True)
        order[sign] = jnp.broadcast_to(inverse, (8, TILE)).astype(jnp.int32)
        ranks.append(jnp.broadcast_to(rank_row, (8, TILE)))
    order_copy = pltpu.make_async_copy(order, order_s, local_sem.at[1])
    order_copy.start()
    forward(3)

    sub = lax.broadcasted_iota(jnp.int32, (8, TILE), 0)
    kept = float(plan.sizes[0])

    def slot_of(sign, hops):
        slot = ranks[sign] + float(plan.region(sign, hops))
        if hops < HOPS and plan.spare[hops]:
            last = plan.region(sign, hops + 1) + plan.sizes[hops] - 1
            slot = jnp.where(ranks[sign] >= kept, float(last) + kept - ranks[sign], slot)
        return slot

    rows = jnp.zeros((8, TILE), jnp.float32)
    for sign in range(2):
        for hop in range(2, HOPS + 1):
            rows = jnp.where(sub == sign * (HOPS - 1) + hop - 1, counts[sign][hop - 1], rows)
    for j in range(1, RING):
        if j == HOPS:
            slot = jnp.where(even, slot_of(0, HOPS), slot_of(1, HOPS))
        else:
            slot = slot_of(0, j) if j < HOPS else slot_of(1, RING - j)
        slot = jnp.where(mask > 0.0, slot, float(plan.zero_slot))
        tab_tx[j] = jnp.where(sub == 0, slot, rows).astype(jnp.int32)
    tab_copies = [
        remote(tab_tx.at[j], tab_rx.at[j], tab_send.at[j], tab_recv.at[j], on_second(j)) for j in range(1, RING)
    ]
    tab_rx[0] = jnp.where(mask > 0.0, flane, float(plan.zero_slot)).astype(jnp.int32)

    for copy in tab_copies:
        start(copy)

    for block in range(0, MINE, CHUNK):
        for sign in range(2):
            first_wait(sign, HOPS - 1, block)
            if block * 2 // MINE == sign:
                start(first(sign, HOPS, block))
    order_copy.wait()
    for block in range(0, MINE, CHUNK):
        first_wait(block * 2 // MINE, HOPS, block)

    early = len(sent)

    numbers = {}
    for sign in range(2):
        for phase, pieces in plan.pieces.items():
            for piece in pieces:
                numbers[sign, phase, piece] = len(numbers)

    def second(sign, phase, piece):
        begin, end, kind = piece
        size = end - begin
        if kind == "own":
            src = lists.at[sign, pl.ds(begin, size)]
        elif kind == "front":
            src = pool.at[pl.ds(plan.region(sign, phase - 1) + begin, size)]
        elif kind == "mixed":
            src = stage.at[sign, pl.ds(plan.staged[phase] + begin, size)]
        elif phase == 2:
            src = lists.at[sign, pl.ds(plan.held - plan.sizes[1] + begin, size)]
        else:
            shift = plan.sizes[phase - 2] - plan.sizes[phase - 1]
            src = pool.at[pl.ds(plan.region(sign, phase - 1) + shift + begin, size)]
        number = numbers[sign, phase, piece]
        dst = pool.at[pl.ds(plan.region(sign, phase) + begin, size)]
        return remote(src, dst, two_send.at[number], two_recv.at[number], on_second(-1 if sign else 1))

    arrived = set()

    def await_slots(sign, phase, begin, end):
        for piece in plan.pieces[phase]:
            if piece[0] < end and begin < piece[1] and (sign, phase, piece) not in arrived:
                arrived.add((sign, phase, piece))
                second(sign, phase, piece).wait_recv()

    def pick(sign, place, rank):
        lists[sign, place] = group[jnp.clip(order_s[sign, 0, rank], 0, GROUP - 1)]

    for piece in plan.pieces[1]:
        for sign in range(2):
            for rank in range(piece[0], piece[1]):
                pick(sign, rank, rank)
            start(second(sign, 1, piece))
    for sign in range(2):
        for i in range(plan.spare[1]):
            pick(sign, plan.held - 1 - i, plan.sizes[0] + i)
    for piece in plan.pieces[2]:
        if piece[2] == "back":
            for sign in range(2):
                start(second(sign, 2, piece))
    own_copy = pltpu.make_async_copy(group, pool.at[pl.ds(0, GROUP)], local_sem.at[2])
    own_copy.start()

    for copy in tab_copies:
        copy.wait_recv()
    tab_copy = pltpu.make_async_copy(tab_rx, tab_s, local_sem.at[3])
    tab_copy.start()

    over = jnp.zeros((8, TILE), jnp.float32)
    left_over = {}
    for sign in range(2):
        moving = [counts[sign][0]]
        for behind in range(1, HOPS):
            table = tab_rx[RING - behind if sign else behind].astype(jnp.float32)
            for hop in (behind, behind + 1):
                if hop > 1:
                    row = sign * (HOPS - 1) + hop - 1
                    moving.append(jnp.broadcast_to(table[row : row + 1], (8, TILE)))
        passed = {2: moving[1], 3: moving[3], 4: moving[5]}
        came = {2: moving[0], 3: moving[1], 4: moving[3]}
        over = jnp.maximum(over, jnp.where(passed[HOPS] > kept, 1.0, 0.0))
        for phase in range(2, HOPS + 1):
            rest = jnp.maximum(came[phase] - kept, 0.0)
            front = jnp.minimum(passed[phase], kept)
            over = jnp.maximum(over, jnp.where(rest > float(plan.spare[phase - 1]), 1.0, 0.0))
            over = jnp.maximum(over, jnp.where(rest + front > float(plan.sizes[phase - 1]), 1.0, 0.0))
            left_over[sign, phase] = rest

    def spread(vote, tx, rx, send, recv, there):
        tx[...] = vote
        copies = [remote(tx, rx.at[j], send.at[j], recv.at[j], there(j)) for j in range(1, RING)]
        for copy in copies:
            start(copy)
        return copies

    def collect(copies, tx, rx):
        for copy in copies:
            copy.wait_recv()
        vote = tx[...]
        for j in range(1, RING):
            vote = jnp.maximum(vote, rx[j])
        return vote

    near_copies = spread(over, near_tx, near_rx, near_send, near_recv, on_second)

    tab_copy.wait()

    def locate(s, carry):
        su, sv, st = source_of(s)
        distance = lax.rem(v - sv + RING, RING)
        for a in range(AB):
            slot = tab_s[distance, 0, su * MINE + a * HELD + st]
            index_s[s * AB + a] = jnp.clip(slot, 0, plan.zero_slot)
        return carry

    lax.fori_loop(0, NS, locate, 0)

    for copy in sent[:early]:
        copy.wait_send()
    del sent[:early]
    for phase in range(2, HOPS + 1):
        size, shift = plan.sizes[phase - 1], plan.sizes[phase - 2] - plan.sizes[phase - 1]
        behind = len(sent)
        for piece in plan.pieces[phase]:
            begin, end, kind = piece
            if phase == 2 and kind == "back":
                continue
            for sign in range(2):
                before = plan.region(sign, phase - 1)
                if kind == "back":
                    await_slots(sign, phase - 1, begin + shift, end + shift)
                else:
                    await_slots(sign, phase - 1, begin, end)
                if kind == "mixed":
                    if phase > 2:
                        await_slots(sign, phase - 1, begin + shift, end + shift)
                    for slot in range(begin, end):
                        if phase > 2:
                            other = pool[before + slot + shift]
                        else:
                            other = lists[sign, plan.held - size + slot]
                        rest = jnp.broadcast_to(left_over[sign, phase][0:1], (TILE, TILE))
                        chosen = jnp.where(
                            rest > float(size - 1 - slot), other.astype(jnp.float32), pool[before + slot].astype(jnp.float32)
                        )
                        stage[sign, plan.staged[phase] + slot] = chosen.astype(jnp.bfloat16)
                start(second(sign, phase, piece))
        if phase == 2:
            vote = collect(near_copies, near_tx, near_rx)
            vote_copies = spread(vote, vote_tx, vote_rx, vote_send, vote_recv, on_first)
        elif phase == 3:
            vote = collect(vote_copies, vote_tx, vote_rx)
            last_copies = spread(vote, last_tx, last_rx, last_send, last_recv, on_ka)
    flag_ref[0] = jnp.max(collect(last_copies, last_tx, last_rx)).astype(jnp.int32)
    for copy in sent[:behind]:
        copy.wait_send()
    del sent[:behind]
    own_copy.wait()
    amp_copy.wait()
    for phase in range(1, HOPS + 1):
        for sign in range(2):
            await_slots(sign, phase, 0, plan.sizes[phase - 1])

    total[...] = jnp.zeros_like(total)

    def multiply(i, carry):
        tiles = [amp[STEP * i + j] for j in range(STEP)]
        bands = [
            jnp.concatenate([pool[index_s[(STEP * i + j) * AB + a]] for j in range(STEP)], axis=0) for a in range(AB)
        ]
        total[...] += jnp.dot(
            jnp.concatenate(tiles, axis=1), jnp.concatenate(bands, axis=1), preferred_element_type=jnp.float32
        )
        return carry

    lax.fori_loop(0, NS // STEP, multiply, 0)

    part_copies = [
        remote(
            total.at[pl.ds(lax.rem(ka + j, KA) * ROWS, ROWS)], part_rx.at[j], part_send.at[j], part_recv.at[j], on_ka(j)
        )
        for j in range(1, KA)
    ]
    for copy in part_copies:
        copy.start()
    for copy in sent:
        copy.wait_send()
    result = total[pl.ds(pl.multiple_of(ka * ROWS, ROWS), ROWS)]
    for j, copy in enumerate(part_copies, 1):
        copy.wait_recv()
        result += part_rx[j]
    out_ref[...] = result
    for copy in part_copies:
        copy.wait_send()


def ladder(plan, number, amplitude, slot_owner, slot_tile, integrals, tile_mask):
    copies = 2 * sum(len(pieces) for pieces in plan.pieces.values())
    scratch = [
        pltpu.SMEM((NS,), jnp.int32),
        pltpu.SMEM((NS,), jnp.int32),
        pltpu.VMEM((1, NS), jnp.int32),
        pltpu.VMEM((1, NS), jnp.int32),
        pltpu.VMEM((AB, HELD), jnp.int32),
        pltpu.VMEM((NS, TILE, TILE), jnp.bfloat16),
        pltpu.VMEM((GROUP, TILE, TILE), jnp.bfloat16),
        pltpu.VMEM((2, plan.held, TILE, TILE), jnp.bfloat16),
        pltpu.VMEM((2, max(plan.stage, 1), TILE, TILE), jnp.bfloat16),
        pltpu.VMEM((plan.slots, TILE, TILE), jnp.bfloat16),
        pltpu.VMEM((RING, 8, TILE), jnp.float32),
        pltpu.VMEM((RING, 8, TILE), jnp.float32),
        pltpu.VMEM((RING, 8, TILE), jnp.float32),
        pltpu.VMEM((2, 8, TILE), jnp.int32),
        pltpu.VMEM((RING, 8, TILE), jnp.int32),
        pltpu.VMEM((RING, 8, TILE), jnp.int32),
        pltpu.VMEM((8, TILE), jnp.float32),
        pltpu.VMEM((RING, 8, TILE), jnp.float32),
        pltpu.VMEM((8, TILE), jnp.float32),
        pltpu.VMEM((RING, 8, TILE), jnp.float32),
        pltpu.VMEM((8, TILE), jnp.float32),
        pltpu.VMEM((KA, 8, TILE), jnp.float32),
        pltpu.SMEM((2, 8, TILE), jnp.int32),
        pltpu.SMEM((RING, 8, TILE), jnp.int32),
        pltpu.SMEM((NS * AB,), jnp.int32),
        pltpu.VMEM((TILE, AB * TILE), jnp.float32),
        pltpu.VMEM((KA, ROWS, AB * TILE), jnp.float32),
        pltpu.SemaphoreType.DMA((11,)),
        pltpu.SemaphoreType.DMA((2 * HOPS * MINE,)),
        pltpu.SemaphoreType.DMA((2 * HOPS * MINE,)),
        pltpu.SemaphoreType.DMA((copies,)),
        pltpu.SemaphoreType.DMA((copies,)),
    ] + [pltpu.SemaphoreType.DMA((RING,)) for _ in range(14)]
    smem, vmem = pl.BlockSpec(memory_space=pltpu.SMEM), pl.BlockSpec(memory_space=pltpu.VMEM)
    hbm = pl.BlockSpec(memory_space=pl.ANY)
    return pl.pallas_call(
        functools.partial(kernel, plan),
        out_shape=(
            jax.ShapeDtypeStruct((ROWS, AB * TILE), jnp.float32),
            jax.ShapeDtypeStruct((1,), jnp.int32),
        ),
        in_specs=[hbm] * 7,
        out_specs=(vmem, smem),
        scratch_shapes=scratch,
        compiler_params=pltpu.CompilerParams(
            collective_id=number, has_side_effects=True, vmem_limit_bytes=32 * 1024 * 1024
        ),
    )(slot_owner, slot_tile, slot_owner[None], slot_tile[None], tile_mask.T, integrals, amplitude)


def local(*arrays):
    result, over = ladder(USUAL, 0, *arrays)
    return lax.cond(over[0] > 0, lambda: ladder(EVERY, 1, *arrays)[0], lambda: result)


def solution(mesh):
    in_specs = (
        P(("pair", "ka"), None, None),
        P(("pair", "ka")),
        P(("pair", "ka")),
        P(("pair", "ka"), None, None),
        P(("pair", "ka"), None),
    )
    out_specs = P(("pair", "ka"), None)
    return jax.shard_map(local, mesh=mesh, in_specs=in_specs, out_specs=out_specs, check_vma=False)
```

```python
import functools

import jax
import jax.numpy as jnp
from jax import lax
from jax.experimental import pallas as pl
from jax.experimental.pallas import tpu as pltpu
from jax.sharding import PartitionSpec as P

MESH = pl.DeviceIdType.MESH

TILE = 128
AB = 2
HELD = 3
NS = 48
RING = 8
KA = 8
MINE = HELD * AB
GROUP = RING * MINE
CHUNK = 1
STEP = 8
ROWS = TILE // KA

HOPS = RING // 2
LONGEST = 4


class Plan:
    def __init__(self, sizes, spare):
        self.sizes, self.spare = sizes, spare
        self.zero_slot = GROUP + 2 * sum(sizes)
        self.slots = self.zero_slot + 1
        self.held = sizes[0] + spare[1]
        self.pieces = {1: self.cut(0, sizes[0], "own")}
        self.staged = {}
        self.stage = 0
        for phase in range(2, HOPS + 1):
            size = sizes[phase - 1]
            mixed, back = size - spare[phase - 1], min(size, sizes[0])
            front = self.cut(0, mixed, "front") + self.cut(mixed, back, "mixed")
            rear = self.cut(back, size, "back")
            self.pieces[phase] = rear + front if phase == 2 else front + rear
            self.staged[phase] = self.stage - mixed
            self.stage += back - mixed

    @staticmethod
    def cut(begin, end, kind):
        count = -(-(end - begin) // LONGEST)
        edges = [begin + (end - begin) * i // count for i in range(count + 1)] if count else []
        return [(a, b, kind) for a, b in zip(edges, edges[1:])]

    def region(self, sign, phase):
        return GROUP + sign * sum(self.sizes) + sum(self.sizes[: phase - 1])


USUAL = Plan((22, 24, 22, 12), (0, 12, 11, 6))
EVERY = Plan((GROUP, GROUP, GROUP, GROUP // 2), (0, 0, 0, 0))


def kernel(
    plan, owner_hbm, tile_hbm, owner_row_hbm, tile_row_hbm, mask_hbm, integrals_ref, amplitude_ref,
    out_ref, flag_ref,
    owner_ref, tile_ref, owner_row, tile_row, mask_ref, amp, group, lists, stage, pool, need_tx, need_rx, mask_rx, order, tab_tx, tab_rx, near_tx, near_rx, vote_tx, vote_rx, last_tx, last_rx,
    order_s, tab_s, index_s, total, part_rx,
    local_sem, one_send, one_recv, two_send, two_recv, need_send, need_recv, mask_send, mask_recv,
    tab_send, tab_recv, near_send, near_recv, vote_send, vote_recv, last_send, last_recv, part_send, part_recv,
):
    pair, ka = lax.axis_index("pair"), lax.axis_index("ka")
    core = lax.rem(ka, 2)
    high, low = lax.div(pair, RING), lax.rem(pair, RING)
    u = high + core * (low - high)
    v = low + core * (high - low)
    stride_u, stride_v = RING - (RING - 1) * core, 1 + (RING - 1) * core

    def on_first(step):
        return (lax.rem(u + step + RING, RING) * stride_u + v * stride_v, ka)

    def on_second(step):
        return (u * stride_u + lax.rem(v + step + RING, RING) * stride_v, ka)

    def on_ka(step):
        return (pair, lax.rem(ka + step, KA))

    load_copies = [
        pltpu.make_async_copy(
            integrals_ref.at[:, :, pl.ds(a * TILE, TILE)],
            group.at[pl.ds(u * MINE + a * HELD, HELD)],
            local_sem.at[4 + a],
        )
        for a in range(AB)
    ]
    for copy in load_copies:
        copy.start()

    small_copies = [
        pltpu.make_async_copy(source, target, local_sem.at[6 + i])
        for i, (source, target) in enumerate(
            (
                (owner_row_hbm, owner_row),
                (tile_row_hbm, tile_row),
                (mask_hbm, mask_ref),
                (owner_hbm, owner_ref),
                (tile_hbm, tile_ref),
            )
        )
    ]
    barrier = pltpu.get_barrier_semaphore()
    for step in range(1, RING):
        for there in (on_first(step), on_second(step), on_ka(step)):
            pl.semaphore_signal(barrier, inc=1, device_id=there, device_id_type=MESH)

    for copy in small_copies:
        copy.start()
    amp_copy = pltpu.make_async_copy(amplitude_ref, amp, local_sem.at[0])

    for copy in load_copies:
        copy.wait()
    pl.semaphore_wait(barrier, 3 * (RING - 1))

    def remote(src, dst, send, recv, there):
        return pltpu.make_async_remote_copy(
            src_ref=src, dst_ref=dst, send_sem=send, recv_sem=recv, device_id=there, device_id_type=MESH
        )

    def first(sign, hop, block, arrival=False):
        behind = lax.rem(u + (hop - 1 + arrival if sign else RING - hop + 1 - arrival), RING)
        ref = group.at[pl.ds(behind * MINE + block, CHUNK)]
        number = (sign * HOPS + hop - 1) * MINE + block
        return remote(ref, ref, one_send.at[number], one_recv.at[number], on_first(-1 if sign else 1))

    def first_wait(sign, hop, block):
        first(sign, hop, block, arrival=True).wait_recv()

    need_copies = [
        remote(need_tx.at[j], need_rx.at[j], need_send.at[j], need_recv.at[j], on_second(j)) for j in range(1, RING)
    ]
    mask_copies = [
        remote(mask_rx.at[0], mask_rx.at[j], mask_send.at[j], mask_recv.at[j], on_first(j)) for j in range(1, RING)
    ]
    sent = []

    def start(copy):
        copy.start()
        sent.append(copy)

    for block in range(0, MINE, CHUNK):
        for sign in range(2):
            start(first(sign, 1, block))

    for copy in small_copies:
        copy.wait()
    lane = lax.broadcasted_iota(jnp.int32, (8, TILE), 1)
    own_mask = jnp.zeros((8, TILE), jnp.float32)
    for t in range(HELD):
        for a in range(AB):
            here = lane == u * MINE + a * HELD + t
            own_mask = jnp.where(here, mask_ref[a : a + 1, t : t + 1].astype(jnp.float32), own_mask)
    mask_rx[0] = own_mask

    slot_lane = lax.broadcasted_iota(jnp.int32, (NS, NS), 1)
    slot_row = lax.broadcasted_iota(jnp.int32, (NS, NS), 0)
    owner_high, owner_low = lax.shift_right_logical(owner_row[...], 3), lax.bitwise_and(owner_row[...], RING - 1)
    owner_u = owner_high + core * (owner_low - owner_high)
    owner_v = owner_low + core * (owner_high - owner_low)
    steps = lax.bitwise_and(owner_v - v, RING - 1)
    target = (steps * TILE + owner_u * MINE + tile_row[...]).astype(jnp.float32)
    target = jnp.sum(jnp.where(slot_lane == slot_row, jnp.broadcast_to(target, (NS, NS)), 0.0), axis=1, keepdims=True)
    ahead = target - lax.broadcasted_iota(jnp.int32, (NS, TILE), 1).astype(jnp.float32)
    for j in range(RING):
        used = jnp.zeros((NS, TILE), jnp.float32)
        for a in range(AB):
            used = jnp.where(ahead == float(j * TILE - a * HELD), 1.0, used)
        need_tx[j] = jnp.broadcast_to(jnp.max(used, axis=0, keepdims=True), (8, TILE))
    for copy in need_copies + mask_copies:
        start(copy)
    amp_copy.start()
    pool[plan.zero_slot] = jnp.zeros((TILE, TILE), jnp.bfloat16)

    def source_of(s):
        owner = owner_ref[s]
        oh, ol = lax.div(owner, RING), lax.rem(owner, RING)
        return oh + core * (ol - oh), ol + core * (oh - ol), tile_ref[s]

    def forward(hop):
        for block in range(0, MINE, CHUNK):
            for sign in range(2):
                first_wait(sign, hop - 1, block)
                start(first(sign, hop, block))

    forward(2)
    forward(3)

    for copy in need_copies + mask_copies:
        copy.wait_recv()
    mask = mask_rx[0]
    for j in range(1, RING):
        mask = jnp.maximum(mask, mask_rx[j])
    even = (lane % 2) == 0
    flane = lane.astype(jnp.float32)
    wide_lane = lax.broadcasted_iota(jnp.int32, (GROUP, TILE), 1)
    wide_row = lax.broadcasted_iota(jnp.int32, (GROUP, TILE), 0)
    far = []
    for sign in range(2):
        reach = jnp.zeros((8, TILE), jnp.float32)
        for distance in range(1, HOPS):
            needed = need_rx[distance if sign else RING - distance] * mask
            reach = jnp.where(needed > 0.0, float(distance), reach)
        far.append(reach)
    opposite = need_rx[HOPS] * mask > 0.0
    far[0] = jnp.where(jnp.logical_and(opposite, even), float(HOPS), far[0])
    far[1] = jnp.where(jnp.logical_and(opposite, jnp.logical_not(even)), float(HOPS), far[1])
    ranks = []
    counts = []
    for sign in range(2):
        counts.append(
            [
                jnp.broadcast_to(
                    jnp.sum(jnp.where(far[sign] >= float(hop), 1.0, 0.0), axis=1, keepdims=True), (8, TILE)
                )
                for hop in range(1, HOPS + 1)
            ]
        )
        key = far[sign] * float(TILE) + (float(TILE - 1) - flane)
        key_row = jnp.broadcast_to(key[0:1], (GROUP, TILE))
        key_col = jnp.sum(jnp.where(wide_lane == wide_row, key_row, 0.0), axis=1, keepdims=True)
        rank_row = jnp.sum(jnp.where(key_col > key_row, 1.0, 0.0), axis=0, keepdims=True)
        rank_col = jnp.sum(jnp.where(key_row > key_col, 1.0, 0.0), axis=1, keepdims=True)
        chosen = jnp.where(rank_col == wide_lane.astype(jnp.float32), wide_row.astype(jnp.float32), 0.0)
        inverse = jnp.sum(chosen, axis=0, keepdims=True)
        order[sign] = jnp.broadcast_to(inverse, (8, TILE)).astype(jnp.int32)
        ranks.append(jnp.broadcast_to(rank_row, (8, TILE)))
    order_copy = pltpu.make_async_copy(order, order_s, local_sem.at[1])
    order_copy.start()

    sub = lax.broadcasted_iota(jnp.int32, (8, TILE), 0)
    kept = float(plan.sizes[0])

    def slot_of(sign, hops):
        slot = ranks[sign] + float(plan.region(sign, hops))
        if hops < HOPS and plan.spare[hops]:
            last = plan.region(sign, hops + 1) + plan.sizes[hops] - 1
            slot = jnp.where(ranks[sign] >= kept, float(last) + kept - ranks[sign], slot)
        return slot

    rows = jnp.zeros((8, TILE), jnp.float32)
    for sign in range(2):
        for hop in range(2, HOPS + 1):
            rows = jnp.where(sub == sign * (HOPS - 1) + hop - 1, counts[sign][hop - 1], rows)
    for j in range(1, RING):
        if j == HOPS:
            slot = jnp.where(even, slot_of(0, HOPS), slot_of(1, HOPS))
        else:
            slot = slot_of(0, j) if j < HOPS else slot_of(1, RING - j)
        slot = jnp.where(mask > 0.0, slot, float(plan.zero_slot))
        tab_tx[j] = jnp.where(sub == 0, slot, rows).astype(jnp.int32)
    tab_copies = [
        remote(tab_tx.at[j], tab_rx.at[j], tab_send.at[j], tab_recv.at[j], on_second(j)) for j in range(1, RING)
    ]
    tab_rx[0] = jnp.where(mask > 0.0, flane, float(plan.zero_slot)).astype(jnp.int32)

    for copy in tab_copies:
        start(copy)

    for block in range(0, MINE, CHUNK):
        for sign in range(2):
            first_wait(sign, HOPS - 1, block)
            if block * 2 // MINE == sign:
                start(first(sign, HOPS, block))
    order_copy.wait()
    for block in range(0, MINE, CHUNK):
        first_wait(block * 2 // MINE, HOPS, block)

    early = len(sent)

    numbers = {}
    for sign in range(2):
        for phase, pieces in plan.pieces.items():
            for piece in pieces:
                numbers[sign, phase, piece] = len(numbers)

    def second(sign, phase, piece):
        begin, end, kind = piece
        size = end - begin
        if kind == "own":
            src = lists.at[sign, pl.ds(begin, size)]
        elif kind == "front":
            src = pool.at[pl.ds(plan.region(sign, phase - 1) + begin, size)]
        elif kind == "mixed":
            src = stage.at[sign, pl.ds(plan.staged[phase] + begin, size)]
        elif phase == 2:
            src = lists.at[sign, pl.ds(plan.held - plan.sizes[1] + begin, size)]
        else:
            shift = plan.sizes[phase - 2] - plan.sizes[phase - 1]
            src = pool.at[pl.ds(plan.region(sign, phase - 1) + shift + begin, size)]
        number = numbers[sign, phase, piece]
        dst = pool.at[pl.ds(plan.region(sign, phase) + begin, size)]
        return remote(src, dst, two_send.at[number], two_recv.at[number], on_second(-1 if sign else 1))

    arrived = set()

    def await_slots(sign, phase, begin, end):
        for piece in plan.pieces[phase]:
            if piece[0] < end and begin < piece[1] and (sign, phase, piece) not in arrived:
                arrived.add((sign, phase, piece))
                second(sign, phase, piece).wait_recv()

    def pick(sign, place, rank):
        lists[sign, place] = group[jnp.clip(order_s[sign, 0, rank], 0, GROUP - 1)]

    for piece in plan.pieces[1]:
        for sign in range(2):
            for rank in range(piece[0], piece[1]):
                pick(sign, rank, rank)
            start(second(sign, 1, piece))
    for sign in range(2):
        for i in range(plan.spare[1]):
            pick(sign, plan.held - 1 - i, plan.sizes[0] + i)
    for piece in plan.pieces[2]:
        if piece[2] == "back":
            for sign in range(2):
                start(second(sign, 2, piece))
    own_copy = pltpu.make_async_copy(group, pool.at[pl.ds(0, GROUP)], local_sem.at[2])
    own_copy.start()

    for copy in tab_copies:
        copy.wait_recv()
    tab_copy = pltpu.make_async_copy(tab_rx, tab_s, local_sem.at[3])
    tab_copy.start()

    over = jnp.zeros((8, TILE), jnp.float32)
    left_over = {}
    for sign in range(2):
        moving = [counts[sign][0]]
        for behind in range(1, HOPS):
            table = tab_rx[RING - behind if sign else behind].astype(jnp.float32)
            for hop in (behind, behind + 1):
                if hop > 1:
                    row = sign * (HOPS - 1) + hop - 1
                    moving.append(jnp.broadcast_to(table[row : row + 1], (8, TILE)))
        passed = {2: moving[1], 3: moving[3], 4: moving[5]}
        came = {2: moving[0], 3: moving[1], 4: moving[3]}
        over = jnp.maximum(over, jnp.where(passed[HOPS] > kept, 1.0, 0.0))
        for phase in range(2, HOPS + 1):
            rest = jnp.maximum(came[phase] - kept, 0.0)
            front = jnp.minimum(passed[phase], kept)
            over = jnp.maximum(over, jnp.where(rest > float(plan.spare[phase - 1]), 1.0, 0.0))
            over = jnp.maximum(over, jnp.where(rest + front > float(plan.sizes[phase - 1]), 1.0, 0.0))
            left_over[sign, phase] = rest

    def spread(vote, tx, rx, send, recv, there):
        tx[...] = vote
        copies = [remote(tx, rx.at[j], send.at[j], recv.at[j], there(j)) for j in range(1, RING)]
        for copy in copies:
            start(copy)
        return copies

    def collect(copies, tx, rx):
        for copy in copies:
            copy.wait_recv()
        vote = tx[...]
        for j in range(1, RING):
            vote = jnp.maximum(vote, rx[j])
        return vote

    near_copies = spread(over, near_tx, near_rx, near_send, near_recv, on_second)

    tab_copy.wait()

    def locate(s, carry):
        su, sv, st = source_of(s)
        distance = lax.rem(v - sv + RING, RING)
        for a in range(AB):
            slot = tab_s[distance, 0, su * MINE + a * HELD + st]
            index_s[s * AB + a] = jnp.clip(slot, 0, plan.zero_slot)
        return carry

    lax.fori_loop(0, NS, locate, 0)

    for copy in sent[:early]:
        copy.wait_send()
    del sent[:early]
    for phase in range(2, HOPS + 1):
        size, shift = plan.sizes[phase - 1], plan.sizes[phase - 2] - plan.sizes[phase - 1]
        behind = len(sent)
        for piece in plan.pieces[phase]:
            begin, end, kind = piece
            if phase == 2 and kind == "back":
                continue
            for sign in range(2):
                before = plan.region(sign, phase - 1)
                if kind == "back":
                    await_slots(sign, phase - 1, begin + shift, end + shift)
                else:
                    await_slots(sign, phase - 1, begin, end)
                if kind == "mixed":
                    if phase > 2:
                        await_slots(sign, phase - 1, begin + shift, end + shift)
                    for slot in range(begin, end):
                        if phase > 2:
                            other = pool[before + slot + shift]
                        else:
                            other = lists[sign, plan.held - size + slot]
                        rest = jnp.broadcast_to(left_over[sign, phase][0:1], (TILE, TILE))
                        chosen = jnp.where(
                            rest > float(size - 1 - slot), other.astype(jnp.float32), pool[before + slot].astype(jnp.float32)
                        )
                        stage[sign, plan.staged[phase] + slot] = chosen.astype(jnp.bfloat16)
                start(second(sign, phase, piece))
        if phase == 2:
            vote = collect(near_copies, near_tx, near_rx)
            vote_copies = spread(vote, vote_tx, vote_rx, vote_send, vote_recv, on_first)
        elif phase == 3:
            vote = collect(vote_copies, vote_tx, vote_rx)
            last_copies = spread(vote, last_tx, last_rx, last_send, last_recv, on_ka)
    flag_ref[0] = jnp.max(collect(last_copies, last_tx, last_rx)).astype(jnp.int32)
    for copy in sent[:behind]:
        copy.wait_send()
    del sent[:behind]
    own_copy.wait()
    amp_copy.wait()
    for phase in range(1, HOPS + 1):
        for sign in range(2):
            await_slots(sign, phase, 0, plan.sizes[phase - 1])

    total[...] = jnp.zeros_like(total)

    def multiply(i, carry):
        tiles = [amp[STEP * i + j] for j in range(STEP)]
        bands = [
            jnp.concatenate([pool[index_s[(STEP * i + j) * AB + a]] for j in range(STEP)], axis=0) for a in range(AB)
        ]
        total[...] += jnp.dot(
            jnp.concatenate(tiles, axis=1), jnp.concatenate(bands, axis=1), preferred_element_type=jnp.float32
        )
        return carry

    lax.fori_loop(0, NS // STEP, multiply, 0)

    part_copies = [
        remote(
            total.at[pl.ds(lax.rem(ka + j, KA) * ROWS, ROWS)], part_rx.at[j], part_send.at[j], part_recv.at[j], on_ka(j)
        )
        for j in range(1, KA)
    ]
    for copy in part_copies:
        copy.start()
    for copy in sent:
        copy.wait_send()
    result = total[pl.ds(pl.multiple_of(ka * ROWS, ROWS), ROWS)]
    for j, copy in enumerate(part_copies, 1):
        copy.wait_recv()
        result += part_rx[j]
    out_ref[...] = result
    for copy in part_copies:
        copy.wait_send()


def ladder(plan, number, amplitude, slot_owner, slot_tile, integrals, tile_mask):
    copies = 2 * sum(len(pieces) for pieces in plan.pieces.values())
    scratch = [
        pltpu.SMEM((NS,), jnp.int32),
        pltpu.SMEM((NS,), jnp.int32),
        pltpu.VMEM((1, NS), jnp.int32),
        pltpu.VMEM((1, NS), jnp.int32),
        pltpu.VMEM((AB, HELD), jnp.int32),
        pltpu.VMEM((NS, TILE, TILE), jnp.bfloat16),
        pltpu.VMEM((GROUP, TILE, TILE), jnp.bfloat16),
        pltpu.VMEM((2, plan.held, TILE, TILE), jnp.bfloat16),
        pltpu.VMEM((2, max(plan.stage, 1), TILE, TILE), jnp.bfloat16),
        pltpu.VMEM((plan.slots, TILE, TILE), jnp.bfloat16),
        pltpu.VMEM((RING, 8, TILE), jnp.float32),
        pltpu.VMEM((RING, 8, TILE), jnp.float32),
        pltpu.VMEM((RING, 8, TILE), jnp.float32),
        pltpu.VMEM((2, 8, TILE), jnp.int32),
        pltpu.VMEM((RING, 8, TILE), jnp.int32),
        pltpu.VMEM((RING, 8, TILE), jnp.int32),
        pltpu.VMEM((8, TILE), jnp.float32),
        pltpu.VMEM((RING, 8, TILE), jnp.float32),
        pltpu.VMEM((8, TILE), jnp.float32),
        pltpu.VMEM((RING, 8, TILE), jnp.float32),
        pltpu.VMEM((8, TILE), jnp.float32),
        pltpu.VMEM((KA, 8, TILE), jnp.float32),
        pltpu.SMEM((2, 8, TILE), jnp.int32),
        pltpu.SMEM((RING, 8, TILE), jnp.int32),
        pltpu.SMEM((NS * AB,), jnp.int32),
        pltpu.VMEM((TILE, AB * TILE), jnp.float32),
        pltpu.VMEM((KA, ROWS, AB * TILE), jnp.float32),
        pltpu.SemaphoreType.DMA((11,)),
        pltpu.SemaphoreType.DMA((2 * HOPS * MINE,)),
        pltpu.SemaphoreType.DMA((2 * HOPS * MINE,)),
        pltpu.SemaphoreType.DMA((copies,)),
        pltpu.SemaphoreType.DMA((copies,)),
    ] + [pltpu.SemaphoreType.DMA((RING,)) for _ in range(14)]
    smem, vmem = pl.BlockSpec(memory_space=pltpu.SMEM), pl.BlockSpec(memory_space=pltpu.VMEM)
    hbm = pl.BlockSpec(memory_space=pl.ANY)
    return pl.pallas_call(
        functools.partial(kernel, plan),
        out_shape=(
            jax.ShapeDtypeStruct((ROWS, AB * TILE), jnp.float32),
            jax.ShapeDtypeStruct((1,), jnp.int32),
        ),
        in_specs=[hbm] * 7,
        out_specs=(vmem, smem),
        scratch_shapes=scratch,
        compiler_params=pltpu.CompilerParams(
            collective_id=number, has_side_effects=True, vmem_limit_bytes=32 * 1024 * 1024
        ),
    )(slot_owner, slot_tile, slot_owner[None], slot_tile[None], tile_mask.T, integrals, amplitude)


def local(*arrays):
    result, over = ladder(USUAL, 0, *arrays)
    return lax.cond(over[0] > 0, lambda: ladder(EVERY, 1, *arrays)[0], lambda: result)


def solution(mesh):
    in_specs = (
        P(("pair", "ka"), None, None),
        P(("pair", "ka")),
        P(("pair", "ka")),
        P(("pair", "ka"), None, None),
        P(("pair", "ka"), None),
    )
    out_specs = P(("pair", "ka"), None)
    return jax.shard_map(local, mesh=mesh, in_specs=in_specs, out_specs=out_specs, check_vma=False)
```
